512 devices in a mesh: dp: 16 (over y, z_hi), fsdp: 32 (over x, z_lo, core).
Axes of the slice: x: 4, y: 8, z: 8 (z_hi: 2, z_lo: 4; z = z_hi * 4 + z_lo), core: 2. Of those that a mesh axis runs over, the one named last changes fastest.
Arguments:
- tokens: bfloat16 [65536, 8192], P(('dp', 'fsdp')), may hold values from -6 to 6
- grad_out: bfloat16 [65536, 512], P(('dp', 'fsdp')), may hold values from -6 to 6
- base_weight: bfloat16 [8192, 512], P('fsdp'), may hold values from -0.0625 to 0.0625
- frozen_down: bfloat16 [16, 8192, 128], P('dp', 'fsdp'), may hold values from -0.0625 to 0.0625
- trained_up: bfloat16 [16, 128, 512], P('dp', None, 'fsdp'), may hold values from -0.5 to 0.5
- tenant_per_group: int32 [16], P('dp'), may hold values from 0 to 15, as said below
- lengths: int32 [16, 32], P('dp', 'fsdp'), may hold values from 32 to 128, as said below
- ranks: int32 [16], replicated, may hold values from 16 to 128, as said below
Outputs:
- projected: bfloat16 [65536, 512], P(('dp', 'fsdp'))
- input_token_gradient: bfloat16 [65536, 8192], P(('dp', 'fsdp'))
- tenant_up_gradient: float32 [16, 128, 512], P('dp', None, 'fsdp')
The draws below stay inside these ranges and needn't reach their ends.
Inputs may be any that keep to these rules, and one draw needn't show every extreme that they name: `tenant_per_group`: exactly one tenant runs on two indices of dp, exactly one on none, every other on one; some index g of dp runs tenant g - 1 (counted round). `lengths`: at least 32 on every device; some device is full in every draw. `ranks`: multiples of 16; some tenant has the largest rank in every draw.
All inputs are finite; a program needn't handle non-finite values.
Results may differ from the reference program's by a relative error of at most 0.003.
Values may be sent and summed in bfloat16 or wider, within the bound.
A program may use at most 64 MiB of HBM per device.

```python
import jax
import jax.numpy as jnp
from jax import lax

D = 8192
VW = 512
R = 128
TOK_DEV = 128
TENANTS = 16
TOKENS = 65536
N_DP = 16
N_FSDP = 32


def draw_tenant_per_group(key, part):
    key = jax.random.fold_in(key, 7)
    first, second, third, fourth = jax.random.split(key, 4)
    order = jax.random.permutation(first, TENANTS).astype(jnp.int32)
    anchor = jax.random.randint(second, (), 0, N_DP).astype(jnp.int32)
    wanted = ((anchor + N_DP - 1) % N_DP).astype(jnp.int32)
    where_wanted = jnp.sum(jnp.where(order == wanted, jnp.arange(N_DP, dtype=jnp.int32), 0)).astype(jnp.int32)
    displaced = order[anchor]
    order = order.at[where_wanted].set(displaced).at[anchor].set(wanted)
    target = ((anchor + jax.random.randint(third, (), 1, N_DP)) % N_DP).astype(jnp.int32)
    source = ((target + jax.random.randint(fourth, (), 1, N_DP)) % N_DP).astype(jnp.int32)
    return order.at[target].set(order[source]).astype(jnp.int32)


def draw_lengths(key, part):
    key = jax.random.fold_in(key, 11)
    first, second = jax.random.split(key)
    values = jax.random.randint(first, (N_DP * N_FSDP,), TOK_DEV // 4, TOK_DEV + 1)
    full_rank_selector = jax.random.randint(second, (), 0, N_DP * N_FSDP)
    values = values.at[full_rank_selector].set(TOK_DEV)
    return values.reshape(N_DP, N_FSDP).astype(jnp.int32)


def draw_ranks(key, part):
    key = jax.random.fold_in(key, 23)
    first, second = jax.random.split(key)
    values = R // 8 * jax.random.randint(first, (TENANTS,), 1, 9)
    full_rank_selector = jax.random.randint(second, (), 0, TENANTS)
    return values.at[full_rank_selector].set(R).astype(jnp.int32)


def level_of(rng, dims, shards, least, high):
    gain = 1.0
    for position, parts in shards:
        heights = jax.random.uniform(jax.random.fold_in(jax.random.fold_in(rng, 6), position), (parts,), jnp.float32, least / len(shards), high / len(shards))
        gain = gain * jnp.repeat(jnp.exp(heights), dims[position] // parts).reshape((-1,) + (1,) * (len(dims) - 1 - position))
    return gain


def gaussian(rng, extent, deviation, limit, cuts=(), held_as=jnp.bfloat16):
    gain = level_of(rng, extent, cuts, -0.22, 0.18) if cuts else 1.0
    array = jax.random.normal(rng, extent, jnp.float32) * deviation * gain
    return jnp.minimum(jnp.maximum(array, -limit), limit).astype(held_as)


def setup_inputs(seed: int = 0) -> dict:
    splits = jax.random.split(jax.random.key(seed), 9)
    tokens = gaussian(splits[0], (TOKENS, D), 1.0, 6.0, ((0, 512),))
    grad_out = gaussian(splits[1], (TOKENS, VW), 1.0, 6.0, ((0, 512),))
    base_weight = gaussian(splits[2], (D, VW), D ** -0.5, 0.0625, ((0, 32),))
    frozen_down = gaussian(splits[3], (TENANTS, D, R), D ** -0.5, 0.0625, ((0, 16), (1, 32)))
    trained_up = gaussian(splits[4], (TENANTS, R, VW), R ** -0.5, 0.5, ((0, 16), (2, 32)))
    tenant_per_group = draw_tenant_per_group(jax.random.fold_in(splits[8], 71), 0)
    lengths = draw_lengths(jax.random.fold_in(splits[8], 71), 0)
    ranks = draw_ranks(jax.random.fold_in(splits[8], 71), 0)
    return dict(tokens=tokens, grad_out=grad_out, base_weight=base_weight, frozen_down=frozen_down, trained_up=trained_up, tenant_per_group=tenant_per_group, lengths=lengths, ranks=ranks)


adapter_alpha_factor = 2.0

def reference(tokens, grad_out, base_weight, frozen_down, trained_up, tenant_per_group, lengths, ranks):
    rows = N_FSDP * TOK_DEV
    grouped_token_rows = tokens.reshape(N_DP, rows, D)
    grad_groups = grad_out.reshape(N_DP, rows, VW)

    def one_group(packed):
        x_rows, dy_rows, tenant, counts = packed
        down = frozen_down[tenant]
        upper = trained_up[tenant]
        adapter_rank = ranks[tenant]
        adapter_scale = adapter_alpha_factor / jnp.sqrt(adapter_rank.astype(jnp.float32))
        rank_live = (jnp.arange(R) < adapter_rank)[None, :]
        row_live = (jnp.arange(TOK_DEV)[None, :] < counts[:, None]).reshape(rows)[:, None]
        masked = jnp.where(row_live, dy_rows, jnp.zeros_like(dy_rows))
        low = jnp.where(rank_live, jnp.dot(x_rows, down, preferred_element_type=jnp.float32), 0.0).astype(jnp.bfloat16)
        base = jnp.dot(x_rows, base_weight, preferred_element_type=jnp.float32)
        out = base + adapter_scale * jnp.dot(low, upper, preferred_element_type=jnp.float32)
        out = jnp.where(row_live, out, 0.0).astype(jnp.bfloat16)
        glow = adapter_scale * jnp.dot(masked, upper.T, preferred_element_type=jnp.float32)
        glow = jnp.where(rank_live, glow, 0.0).astype(jnp.bfloat16)
        gx = jnp.dot(masked, base_weight.T, preferred_element_type=jnp.float32) + jnp.dot(glow, down.T, preferred_element_type=jnp.float32)
        gup = adapter_scale * jnp.dot(low.T, masked, preferred_element_type=jnp.float32)
        return (out, gx.astype(jnp.bfloat16), gup)
    outs, grads, partials = lax.map(one_group, (grouped_token_rows, grad_groups, tenant_per_group, lengths))
    tenant_up_gradient = jnp.zeros((TENANTS, R, VW), jnp.float32).at[tenant_per_group].add(partials)
    return (outs.reshape(TOKENS, VW), grads.reshape(TOKENS, D), tenant_up_gradient)
```

```python
import functools

import jax
import jax.numpy as jnp
from jax import lax
from jax.experimental import pallas as pl
from jax.experimental.pallas import tpu as pltpu
from jax.sharding import PartitionSpec as P

adapter_alpha_factor = 2.0

MESH = pl.DeviceIdType.MESH
BF, F32 = jnp.bfloat16, jnp.float32

NX = 4
NZL = 4
NZ = 8
N_FSDP = 32
RW = 256
VW = 512
R = 128
TOK = 128
CB = VW // N_FSDP
AR = RW + CB
AH = 144
H1 = 128
PARTS = ((0, H1, H1 // 2), (H1, RW, H1 + (RW - H1) // 2))
REL = (0, 1, 3, 2)


def dot_nn(a, b):
    return lax.dot_general(a, b, (((1,), (0,)), ((), ())), preferred_element_type=F32)


def dot_nt(a, b):
    return lax.dot_general(a, b, (((1,), (1,)), ((), ())), preferred_element_type=F32)


def kernel(
    n_dp, tok_hbm, grad_hbm, w_hbm, a_hbm, bt_hbm, tid_s, len_s, rank_s,
    proj_ref, gx_ref, gup_ref,
    tok, masked, glow, w, a, a_own, bt_own, m_out, m_in, q_out, bt, rs_out, rs_in, dp_out, dp_in,
    proj_acc, low_acc,
    load_sem, sw_ici, sw_d2d, sa_ici, sa_d2d, s_hop, rw_ici, rw_d2d, ra_z, ra_x, ra_dz, ra_dx, r_hop,
):
    pr = RW // n_dp
    g = lax.axis_index("dp")
    f = lax.axis_index("fsdp")
    y, zh = g // 2, g % 2
    x, zl, c = f // 8, (f // 2) % 4, f % 2
    z = zh * NZL + zl

    def at(dx, dz):
        xx, zz = (x + dx) % NX, (z + dz) % NZ
        return (y * 2 + zz // NZL, xx * 8 + (zz % NZL) * 2 + c)

    partner = (g, f + 1 - 2 * c)
    x_up, x_dn = at(1, 0), at(NX - 1, 0)
    z_up, z_dn = at(0, 1), at(0, NZ - 1)

    loads = [
        pltpu.make_async_copy(w_hbm, w.at[pl.ds(pl.multiple_of(f * RW, RW), RW)], load_sem.at[0]),
        pltpu.make_async_copy(a_hbm, a_own, load_sem.at[1]),
        pltpu.make_async_copy(bt_hbm, bt_own, load_sem.at[2]),
        pltpu.make_async_copy(grad_hbm, masked, load_sem.at[3]),
        pltpu.make_async_copy(tok_hbm, tok, load_sem.at[4]),
    ]
    for load in loads:
        load.start()

    barrier = pltpu.get_barrier_semaphore()

    def greet(dev):
        pl.semaphore_signal(barrier, inc=1, device_id=dev, device_id_type=MESH)

    greet(z_up)
    greet(z_dn)

    def greet_fsdp(k, _):
        greet((g, (f + k) % N_FSDP))
        return 0

    def greet_dp(k, _):
        greet(((g + k) % n_dp, f))
        return 0

    lax.fori_loop(1, N_FSDP, greet_fsdp, 0)
    lax.fori_loop(1, n_dp, greet_dp, 0)

    loads[1].wait()
    loads[2].wait()
    tenant = tid_s[0]
    rank = rank_s[tenant]
    tid_tile = jnp.full((16, R), tenant, jnp.int32).astype(F32).astype(BF)

    def pack(j, _):
        m_out[j, 0:pr] = a_own[pl.ds(pl.multiple_of(j * pr, pr), pr)]
        m_out[j, pr : pr + CB] = bt_own[...]
        m_out[j, pr + CB : pr + CB + 16] = tid_tile
        return 0

    lax.fori_loop(0, n_dp, pack, 0)
    m_in[g] = m_out[g]

    scale = adapter_alpha_factor / jnp.sqrt(jnp.full((1, R), rank, jnp.int32).astype(F32))
    scale_wide = adapter_alpha_factor / jnp.sqrt(jnp.full((1, VW), rank, jnp.int32).astype(F32))
    rank_live = lax.broadcasted_iota(jnp.int32, (TOK, R), 1) < rank
    row_live = lax.broadcasted_iota(jnp.int32, (TOK, VW), 0) < len_s[0, 0]
    loads[3].wait()
    masked[...] = jnp.where(row_live, masked[...].astype(F32), 0.0).astype(BF)
    proj_acc[...] = jnp.zeros_like(proj_acc)
    low_acc[...] = jnp.zeros_like(low_acc)
    loads[0].wait()
    pl.semaphore_wait(barrier, N_FSDP - 1 + n_dp - 1 + 2)

    def remote(src, dst, send, recv, dev):
        return pltpu.make_async_remote_copy(
            src_ref=src, dst_ref=dst, send_sem=send, recv_sem=recv, device_id=dev, device_id_type=MESH
        )

    def arrived(ref, sem):
        remote(ref, ref, s_hop.at[0], sem, partner).wait_recv()

    def sent(ref, sem):
        remote(ref, ref, sem, r_hop.at[0], partner).wait_send()

    def hop1(k, _):
        j = (g + k) % n_dp
        remote(m_out.at[j], m_in.at[g], s_hop.at[0], r_hop.at[0], (j, f)).start()
        return 0

    lax.fori_loop(1, n_dp, hop1, 0)

    def place(dx, dz):
        return ((x + dx) % NX) * 8 + ((zl + dz) % NZL) * 2 + c

    def w_rows(dx, dz, lo, hi):
        return w.at[pl.ds(pl.multiple_of(place(dx, dz) * RW + lo, 16), hi - lo)]

    def span(stream, part):
        lo, hi, mid = PARTS[stream]
        return {"all": (lo, hi), "lo": (lo, mid), "hi": (mid, hi)}[part]

    def slot(dx, dz):
        return (dx % 4) * 4 + dz % 4

    def w_send(stream, dx, dz, part, axis, step):
        ref = w_rows(dx, dz, *span(stream, part))
        if axis == "x":
            dev = x_up if step == 1 else x_dn
            there = slot(dx - step, dz)
        else:
            dev = z_up if step == 1 else z_dn
            there = slot(dx, dz - step)
        remote(ref, ref, sw_ici, rw_ici.at[stream, there, int(part == "hi")], dev).start()

    def w_d2d(stream, dx, dz, part):
        ref = w_rows(dx, dz, *span(stream, part))
        remote(ref, ref, sw_d2d, rw_d2d.at[stream, slot(dx, dz), int(part == "hi")], partner).start()

    def w_wait(stream, dx, dz, part):
        arrived(w_rows(dx, dz, *span(stream, part)), rw_ici.at[stream, slot(dx, dz), int(part == "hi")])
        w_d2d(stream, dx, dz, part)

    def other_rows(dx, dz, lo, hi):
        return w.at[pl.ds(pl.multiple_of((place(dx, dz) + 1 - 2 * c) * RW + lo, 16), hi - lo)]

    def w_other(dx, dz):
        for stream in (0, 1):
            for part in parts_of(stream, dx, dz):
                arrived(other_rows(dx, dz, *span(stream, part)), rw_d2d.at[stream, slot(dx, dz), int(part == "hi")])

    def parts_of(stream, dx, dz):
        last = 0
        if stream == 0:
            last = dz if dz else dx
        else:
            last = dx if dx else dz
        return ("lo", "hi") if last == 2 else ("all",)

    def pick(stream, p, q):
        return (p, q) if stream == 0 else (q, p)

    axes = (("x", "z"), ("z", "x"))

    def first_start():
        for stream in (0, 1):
            for step in (1, -1):
                w_send(stream, 0, 0, "all", axes[stream][0], step)
        for stream in (0, 1):
            w_d2d(stream, 0, 0, "all")

    def second_start(p):
        for stream in (0, 1):
            for step in (1, -1):
                w_send(stream, *pick(stream, p, 0), "all", axes[stream][1], step)

    def first_wait(p):
        for stream in (0, 1):
            if p == 2:
                for part in ("lo", "hi"):
                    w_wait(stream, *pick(stream, p, 0), part)
            else:
                w_wait(stream, *pick(stream, p, 0), "all")
                if p == 3:
                    w_send(stream, *pick(stream, p, 0), "lo", axes[stream][0], 1)
                else:
                    w_send(stream, *pick(stream, p, 0), "hi", axes[stream][0], -1)

    def second_wait(p):
        for stream in (0, 1):
            for q in (3, 1):
                w_wait(stream, *pick(stream, p, q), "all")
                if q == 3:
                    w_send(stream, *pick(stream, p, q), "lo", axes[stream][1], 1)
                else:
                    w_send(stream, *pick(stream, p, q), "hi", axes[stream][1], -1)

    def last_wait(p):
        for stream in (0, 1):
            for part in ("lo", "hi"):
                w_wait(stream, *pick(stream, p, 2), part)

    def choose(tile, first, rows):
        total = jnp.zeros((rows, R), F32)
        for u in range(n_dp):
            total = total + jnp.where(tile == u, m_in[u, first : first + rows].astype(F32), 0.0)
        return total.astype(BF)

    def tile_of(k, rows):
        t = m_in[k, pr + CB : pr + CB + 16].astype(F32)
        return jnp.broadcast_to(t[0:1], (rows, R)) if rows != 16 else t

    def second_hop():
        arrived(m_in.at[pl.ds(0, n_dp - 1)], r_hop.at[0])

        def hop2(k, _):
            j = (g + k) % n_dp
            q_out[j] = choose(tile_of(j, pr), 0, pr)
            mine = a.at[f, pl.ds(pl.multiple_of(g * pr, pr), pr)]
            remote(q_out.at[j], mine, s_hop.at[1], r_hop.at[1], (j, f)).start()
            return 0

        lax.fori_loop(1, n_dp, hop2, 0)
        a[f, pl.ds(pl.multiple_of(g * pr, pr), pr)] = choose(tile_of(g, pr), 0, pr)
        a[f, RW:AR] = choose(tile_of(g, CB), pr, CB)

    def z_near(s):
        return (zl, zl + 1 - 2 * (zl % 2), zl + 2 - 4 * (zl // 2), 3 - zl)[s]

    def a_slot(dx, s):
        return ((x + dx) % NX) * 8 + z_near(s) * 2 + c

    def a_other(dx, s):
        return a_slot(dx, s) + 1 - 2 * c

    def a_d2d(ref, sem):
        remote(ref, ref, sa_d2d, sem, partner).start()

    def a_start():
        arrived(a.at[f, pl.ds(0, (n_dp - 1) * pr)], r_hop.at[1])
        ref = a.at[f]
        for s in (1, 2, 3):
            remote(ref, ref, sa_ici, ra_z.at[s], (g, a_slot(0, s))).start()
        a_d2d(ref, ra_dz.at[0])
        a_along_x(0)

    def a_along_x(s):
        ref = a.at[a_slot(0, s)]
        remote(ref, ref, sa_ici, ra_x.at[s, 0], x_up).start()
        remote(ref, ref, sa_ici, ra_x.at[s, 1], x_dn).start()

    def a_z_wait(s):
        ref = a.at[a_slot(0, s)]
        arrived(ref, ra_z.at[s])
        a_d2d(ref, ra_dz.at[s])
        a_along_x(s)

    def a_x_wait(s):
        dn = a.at[a_slot(3, s)]
        arrived(dn, ra_x.at[s, 0])
        part = a.at[a_slot(3, s), pl.ds(0, AH)]
        remote(part, part, sa_ici, ra_x.at[s, 2], x_up).start()
        a_d2d(dn, ra_dx.at[s, 0])
        up = a.at[a_slot(1, s)]
        arrived(up, ra_x.at[s, 1])
        part = a.at[a_slot(1, s), pl.ds(AH, AR - AH)]
        remote(part, part, sa_ici, ra_x.at[s, 3], x_dn).start()
        a_d2d(up, ra_dx.at[s, 1])

    def a_x_last(s):
        lo = a.at[a_slot(2, s), pl.ds(0, AH)]
        arrived(lo, ra_x.at[s, 2])
        a_d2d(lo, ra_dx.at[s, 2])
        hi = a.at[a_slot(2, s), pl.ds(AH, AR - AH)]
        arrived(hi, ra_x.at[s, 3])
        a_d2d(hi, ra_dx.at[s, 3])

    def a_others():
        for s in range(4):
            arrived(a.at[a_other(0, s)], ra_dz.at[s])
            arrived(a.at[a_other(3, s)], ra_dx.at[s, 0])
            arrived(a.at[a_other(1, s)], ra_dx.at[s, 1])
            arrived(a.at[a_other(2, s), pl.ds(0, AH)], ra_dx.at[s, 2])
            arrived(a.at[a_other(2, s), pl.ds(AH, AR - AH)], ra_dx.at[s, 3])

    def cols(p):
        return pl.ds(pl.multiple_of(p * 2 * RW, 2 * RW), 2 * RW)

    def forward(p):
        proj_acc[...] += dot_nn(tok[:, cols(p)], w[cols(p)])

    def backward(p):
        base = dot_nt(masked[...], w[cols(p)])
        low_part = jnp.concatenate([dot_nt(glow[...], a[2 * p + k, 0:RW]) for k in (0, 1)], axis=1)
        gx_ref[:, cols(p)] = (base + low_part).astype(BF)

    def over(pairs, body):
        code_x = sum((dx % 4) * 4**i for i, (dx, dz) in enumerate(pairs))
        code_z = sum((dz % 4) * 4**i for i, (dx, dz) in enumerate(pairs))

        def step(_, carry):
            cx, cz = carry
            body(((x + cx % 4) % NX) * 4 + (zl + cz % 4) % NZL)
            return cx // 4, cz // 4

        lax.fori_loop(0, len(pairs), step, (jnp.int32(code_x), jnp.int32(code_z)))

    def others(pairs):
        for dx, dz in pairs:
            w_other(dx, dz)

    def both(p):
        forward(p)
        backward(p)

    first_start()
    second_hop()
    second_start(0)
    first_wait(3)
    first_wait(1)
    a_start()
    second_start(3)
    second_start(1)
    first_wait(2)
    second_start(2)
    for s in (1, 2, 3):
        a_z_wait(s)
    loads[4].wait()
    group = [(0, 0)]
    others(group)
    over(group, forward)
    second_wait(0)
    for s in range(4):
        a_x_wait(s)
    early = [(1, 0), (3, 0), (0, 1), (0, 3)]
    others(early)
    over(early, forward)
    for s in range(4):
        a_x_last(s)
    second_wait(3)
    a_others()

    for k in range(N_FSDP):
        bt[k * CB : (k + 1) * CB] = a[k, RW:AR]
    glow[...] = jnp.where(rank_live, scale * dot_nn(masked[...], bt[...]), 0.0).astype(BF)

    def low_step(k, _):
        low_acc[...] += dot_nn(tok[:, pl.ds(pl.multiple_of(k * RW, RW), RW)], a[k, 0:RW])
        return 0

    lax.fori_loop(0, N_FSDP, low_step, 0)
    low = jnp.where(rank_live, low_acc[...], 0.0).astype(BF)
    rs_out[...] = (
        lax.dot_general(masked[...], low, (((0,), (0,)), ((), ())), preferred_element_type=F32) * scale
    ).reshape(N_FSDP, CB, R)
    rs_in[f] = rs_out[f]

    def scatter(k, _):
        j = (f + k) % N_FSDP
        remote(rs_out.at[j], rs_in.at[f], s_hop.at[2], r_hop.at[2], (g, j)).start()
        return 0

    lax.fori_loop(1, N_FSDP, scatter, 0)
    proj_acc[...] += scale_wide * dot_nt(low, bt[...])

    second_wait(1)
    second_wait(2)
    over([(0, 0)] + early, backward)
    middle = [(1, 1), (1, 3), (3, 1), (3, 3)]
    others(middle)
    over(middle, both)

    arrived(rs_in.at[pl.ds(0, N_FSDP - 1)], r_hop.at[2])
    total = rs_in[0]
    for k in range(1, N_FSDP):
        total = total + rs_in[k]
    dp_out[...] = total
    dp_in[g] = total

    def spread(k, _):
        remote(dp_out, dp_in.at[g], s_hop.at[3], r_hop.at[3], ((g + k) % n_dp, f)).start()
        return 0

    lax.fori_loop(1, n_dp, spread, 0)

    last_wait(0)
    last_wait(3)
    last_wait(1)
    late = [(2, 0), (0, 2), (2, 1), (1, 2), (2, 3), (3, 2)]
    others(late)
    over(late, both)
    last_wait(2)
    others([(2, 2)])
    over([(2, 2)], both)
    proj_ref[...] = jnp.where(row_live, proj_acc[...], 0.0).astype(BF)

    arrived(dp_in.at[pl.ds(0, n_dp - 1)], r_hop.at[3])
    total = jnp.zeros((CB, R), F32)
    for k in range(n_dp):
        total = total + jnp.where(tile_of(k, CB) == g.astype(F32), dp_in[k], 0.0)
    gup_ref[...] = total

    sent(w.at[pl.ds(0, 15 * RW)], sw_ici)
    sent(w.at[pl.ds(0, 16 * RW)], sw_d2d)
    sent(a.at[pl.ds(0, 15)], sa_ici)
    sent(a.at[pl.ds(0, 16)], sa_d2d)
    sent(m_in.at[pl.ds(0, n_dp - 1)], s_hop.at[0])
    sent(q_out.at[pl.ds(0, n_dp - 1)], s_hop.at[1])
    sent(rs_in.at[pl.ds(0, N_FSDP - 1)], s_hop.at[2])
    sent(dp_in.at[pl.ds(0, n_dp - 1)], s_hop.at[3])


def per_device(
    tokens, grad_out, base_weight, frozen_down, trained_up, tenant_per_group, lengths, ranks
):
    n_dp = ranks.shape[0]
    pr = RW // n_dp
    hbm = pl.BlockSpec(memory_space=pl.ANY)
    smem = pl.BlockSpec(memory_space=pltpu.SMEM)
    vmem = pl.BlockSpec(memory_space=pltpu.VMEM)
    dma = pltpu.SemaphoreType.DMA
    projected, grad_x, up = pl.pallas_call(
        functools.partial(kernel, n_dp),
        out_shape=(
            jax.ShapeDtypeStruct((TOK, VW), BF),
            jax.ShapeDtypeStruct((TOK, N_FSDP * RW), BF),
            jax.ShapeDtypeStruct((CB, R), F32),
        ),
        in_specs=[hbm] * 5 + [smem] * 3,
        out_specs=(vmem, vmem, vmem),
        scratch_shapes=[
            pltpu.VMEM((TOK, N_FSDP * RW), BF),
            pltpu.VMEM((TOK, VW), BF),
            pltpu.VMEM((TOK, R), BF),
            pltpu.VMEM((N_FSDP * RW, VW), BF),
            pltpu.VMEM((N_FSDP, AR, R), BF),
            pltpu.VMEM((RW, R), BF),
            pltpu.VMEM((CB, R), BF),
            pltpu.VMEM((n_dp, pr + CB + 16, R), BF),
            pltpu.VMEM((n_dp, pr + CB + 16, R), BF),
            pltpu.VMEM((n_dp, pr, R), BF),
            pltpu.VMEM((VW, R), BF),
            pltpu.VMEM((N_FSDP, CB, R), F32),
            pltpu.VMEM((N_FSDP, CB, R), F32),
            pltpu.VMEM((CB, R), F32),
            pltpu.VMEM((n_dp, CB, R), F32),
            pltpu.VMEM((TOK, VW), F32),
            pltpu.VMEM((TOK, R), F32),
            dma((5,)),
            dma,
            dma,
            dma,
            dma,
            dma((4,)),
            dma((2, 16, 2)),
            dma((2, 16, 2)),
            dma((4,)),
            dma((4, 4)),
            dma((4,)),
            dma((4, 4)),
            dma((4,)),
        ],
        compiler_params=pltpu.CompilerParams(
            collective_id=0, has_side_effects=True, vmem_limit_bytes=40 * 1024 * 1024
        ),
        cost_estimate=pl.CostEstimate(
            flops=2 * 2 * TOK * N_FSDP * RW * (VW + R), bytes_accessed=5 * 1024 * 1024, transcendentals=0
        ),
        name="gather_and_multiply",
    )(
        tokens, grad_out, base_weight, frozen_down[0], jnp.swapaxes(trained_up[0], 0, 1),
        tenant_per_group, lengths, ranks,
    )
    return projected, grad_x, jnp.swapaxes(up, 0, 1)[None]


def solution(mesh):
    placed = (
        P(("dp", "fsdp"), None),
        P(("dp", "fsdp"), None),
        P("fsdp", None),
        P("dp", "fsdp", None),
        P("dp", None, "fsdp"),
        P("dp"),
        P("dp", "fsdp"),
        P(),
    )
    return jax.shard_map(
        per_device,
        mesh=mesh,
        in_specs=placed,
        out_specs=(P(("dp", "fsdp"), None), P(("dp", "fsdp"), None), P("dp", None, "fsdp")),
        check_vma=False,
    )
```

```python
import functools

import jax
import jax.numpy as jnp
from jax import lax
from jax.experimental import pallas as pl
from jax.experimental.pallas import tpu as pltpu
from jax.sharding import PartitionSpec as P

adapter_alpha_factor = 2.0

MESH = pl.DeviceIdType.MESH
BF, F32 = jnp.bfloat16, jnp.float32

NX = 4
NZL = 4
NZ = 8
N_FSDP = 32
RW = 256
VW = 512
R = 128
TOK = 128
N_CHIP = N_FSDP // 2
CB = VW // N_FSDP
AH = RW // 2
SIDE = 80


def dot_nn(a, b):
    return lax.dot_general(a, b, (((1,), (0,)), ((), ())), preferred_element_type=F32)


def dot_nt(a, b):
    return lax.dot_general(a, b, (((1,), (1,)), ((), ())), preferred_element_type=F32)


def kernel(
    n_dp, tok_hbm, grad_hbm, w_hbm, a_hbm, bt_hbm, tid_s, len_s, rank_s,
    proj_ref, gx_ref, gup_ref,
    tok, masked, glow, w, a, tid_all, a_in, b_in, q_out, bt_in, bt, rs_out, rs_mid, rs_in, dp_out, dp_in,
    proj_acc, low_acc,
    load_sem, sw_ici, sw_d2d, sa_ici, sa_d2d, s_hop, rw_ici, rw_d2d, ra_z, ra_x, ra_dz, ra_dx, r_hop,
):
    n_y = n_dp // 2
    pr = RW // n_y
    g = lax.axis_index("dp")
    f = lax.axis_index("fsdp")
    y, zh = g // 2, g % 2
    x, zl, c = f // 8, (f // 2) % 4, f % 2
    z = zh * NZL + zl

    def at(dx, dz):
        xx, zz = (x + dx) % NX, (z + dz) % NZ
        return (y * 2 + zz // NZL, xx * 8 + (zz % NZL) * 2 + c)

    partner = (g, f + 1 - 2 * c)
    x_up, x_dn = at(1, 0), at(NX - 1, 0)
    z_up, z_dn = at(0, 1), at(0, NZ - 1)
    y_up, y_dn = ((y + 1) % n_y * 2 + zh, f), ((y + n_y - 1) % n_y * 2 + zh, f)

    loads = [
        pltpu.make_async_copy(w_hbm, w.at[pl.ds(pl.multiple_of(f * RW, RW), RW)], load_sem.at[0]),
        pltpu.make_async_copy(a_hbm.at[pl.ds(pl.multiple_of(y * pr, pr), pr)], a_in.at[g], load_sem.at[1]),
        pltpu.make_async_copy(bt_hbm, b_in.at[g], load_sem.at[2]),
        pltpu.make_async_copy(grad_hbm, masked, load_sem.at[3]),
        pltpu.make_async_copy(tok_hbm, tok, load_sem.at[4]),
    ]

    by_distance = sorted(range(n_y), key=lambda d: -min(d, n_y - d))
    dp_peers = [((y + d) % n_y * 2 + (zh + e) % 2, f) for e in (1, 0) for d in by_distance if d or e]
    chip = f // 2

    def chip_peer(k):
        return (g, (chip + k) % N_CHIP * 2 + c)

    barrier = pltpu.get_barrier_semaphore()

    def greet(dev):
        pl.semaphore_signal(barrier, inc=1, device_id=dev, device_id_type=MESH)

    for peer in dp_peers:
        greet(peer)

    def greet_chips(k, _):
        greet(chip_peer(k))
        return 0

    lax.fori_loop(1, N_CHIP, greet_chips, 0)
    greet(z_up)
    greet(z_dn)
    greet(partner)
    for load in loads:
        load.start()
    tenant = tid_s[0]
    rank = rank_s[tenant]
    tid_all[g] = jnp.full((1, R), tenant, jnp.int32)

    def remote(src, dst, send, recv, dev):
        return pltpu.make_async_remote_copy(
            src_ref=src, dst_ref=dst, send_sem=send, recv_sem=recv, device_id=dev, device_id_type=MESH
        )

    def arrived(ref, sem):
        remote(ref, ref, s_hop.at[0], sem, partner).wait_recv()

    def sent(ref, sem):
        remote(ref, ref, sem, r_hop.at[0], partner).wait_send()

    pl.semaphore_wait(barrier, n_dp - 1 + N_CHIP - 1 + 3)

    for j, _ in dp_peers:
        rows = a_hbm.at[pl.ds(pl.multiple_of(j // 2 * pr, pr), pr)]
        remote(rows, a_in.at[g], s_hop.at[0], r_hop.at[0], (j, f)).start()
        remote(tid_all.at[g], tid_all.at[g], s_hop.at[5], r_hop.at[5], (j, f)).start()

    def hop1_b():
        for peer in dp_peers:
            remote(bt_hbm, b_in.at[g], s_hop.at[4], r_hop.at[4], peer).start()

    def prepare():
        loads[3].wait()
        masked[...] = jnp.where(row_live, masked[...].astype(F32), 0.0).astype(BF)
        proj_acc[...] = jnp.zeros_like(proj_acc)
        low_acc[...] = jnp.zeros_like(low_acc)

    scale = adapter_alpha_factor / jnp.sqrt(jnp.full((1, R), rank, jnp.int32).astype(F32))
    scale_wide = adapter_alpha_factor / jnp.sqrt(jnp.full((1, VW), rank, jnp.int32).astype(F32))
    rank_live = lax.broadcasted_iota(jnp.int32, (TOK, R), 1) < rank
    row_live = lax.broadcasted_iota(jnp.int32, (TOK, VW), 0) < len_s[0, 0]

    def place(dx, dz):
        return ((x + dx) % NX) * 8 + ((zl + dz) % NZL) * 2 + c

    def rows_at(where, lo, first, last):
        return w.at[pl.ds(pl.multiple_of(where * RW + lo + first, 16), last - first)]

    def w_rows(dx, dz, *span):
        return rows_at(place(dx, dz), *span)

    odd = y % 2
    low_row = (odd * (RW - SIDE), SIDE, (1 - odd) * (RW - SIDE))
    size = (SIDE, RW - 2 * SIDE, SIDE)
    half = (48, 48, 0)

    def span(stream, part):
        lo = low_row[stream]
        ends = {"all": (0, size[stream]), "lo": (0, half[stream]), "hi": (half[stream], size[stream])}[part]
        return lo, ends[0], ends[1]

    def slot(dx, dz):
        return (dx % 4) * 4 + dz % 4

    def w_send(stream, dx, dz, part, axis, step):
        ref = w_rows(dx, dz, *span(stream, part))
        if axis == "x":
            dev = x_up if step == 1 else x_dn
            there = slot(dx - step, dz)
        else:
            dev = z_up if step == 1 else z_dn
            there = slot(dx, dz - step)
        remote(ref, ref, sw_ici, rw_ici.at[stream, there, int(part == "hi")], dev).start()

    def w_d2d(stream, dx, dz, part):
        ref = w_rows(dx, dz, *span(stream, part))
        remote(ref, ref, sw_d2d, rw_d2d.at[stream, slot(dx, dz), int(part == "hi")], partner).start()

    def w_wait(stream, dx, dz, part):
        arrived(w_rows(dx, dz, *span(stream, part)), rw_ici.at[stream, slot(dx, dz), int(part == "hi")])
        w_d2d(stream, dx, dz, part)

    def other_rows(dx, dz, *span):
        return rows_at(place(dx, dz) + 1 - 2 * c, *span)

    def w_other(dx, dz):
        if (dx, dz) == (0, 0):
            arrived(other_rows(0, 0, 0, 0, RW), rw_d2d.at[0, 0, 0])
            return
        for stream in (0, 1, 2):
            for part in parts_of(stream, dx, dz):
                arrived(other_rows(dx, dz, *span(stream, part)), rw_d2d.at[stream, slot(dx, dz), int(part == "hi")])

    def w_side(dx, dz):
        ref = w_rows(dx, dz, *span(0, "all"))
        dev = y_dn if (dx + dz) % 2 else y_up
        remote(ref, ref, sw_ici, rw_ici.at[2, slot(dx, dz), 0], dev).start()

    def w_side_wait(dx, dz):
        arrived(w_rows(dx, dz, *span(2, "all")), rw_ici.at[2, slot(dx, dz), 0])
        w_d2d(2, dx, dz, "all")

    def sides(pairs):
        for dx, dz in pairs:
            w_side_wait(dx, dz)

    def parts_of(stream, dx, dz):
        last = 0
        if stream == 1:
            last = dz if dz else dx
        elif stream == 0:
            last = dx if dx else dz
        return ("lo", "hi") if last == 2 else ("all",)

    def pick(stream, p, q):
        return (p, q) if stream == 1 else (q, p)

    axes = (("z", "x"), ("x", "z"))

    def first_start():
        for stream in (0, 1):
            for step in (1, -1):
                w_send(stream, 0, 0, "all", axes[stream][0], step)
        ref = w_rows(0, 0, 0, 0, RW)
        remote(ref, ref, sw_d2d, rw_d2d.at[0, 0, 0], partner).start()

    def second_start(p):
        for stream in (0, 1):
            for step in (1, -1):
                w_send(stream, *pick(stream, p, 0), "all", axes[stream][1], step)

    def first_wait(p):
        for stream in (0, 1):
            if p == 2:
                for part in ("lo", "hi"):
                    w_wait(stream, *pick(stream, p, 0), part)
                if stream == 0:
                    w_side(*pick(stream, p, 0))
            else:
                w_wait(stream, *pick(stream, p, 0), "all")
                if stream == 0:
                    w_side(*pick(stream, p, 0))
                if p == 3:
                    w_send(stream, *pick(stream, p, 0), "lo", axes[stream][0], 1)
                else:
                    w_send(stream, *pick(stream, p, 0), "hi", axes[stream][0], -1)

    def second_wait(p):
        for stream in (0, 1):
            for q in (3, 1):
                w_wait(stream, *pick(stream, p, q), "all")
                if stream == 0:
                    w_side(*pick(stream, p, q))
                if q == 3:
                    w_send(stream, *pick(stream, p, q), "lo", axes[stream][1], 1)
                else:
                    w_send(stream, *pick(stream, p, q), "hi", axes[stream][1], -1)

    def last_wait(p):
        for stream in (0, 1):
            for part in ("lo", "hi"):
                w_wait(stream, *pick(stream, p, 2), part)
            if stream == 0:
                w_side(*pick(stream, p, 2))

    def choose(k):
        tile = jnp.broadcast_to(tid_all[k], (pr, R))
        total = jnp.zeros((pr, R), F32)
        for u in range(n_dp):
            total = total + jnp.where(tile == u, a_in[u].astype(F32), 0.0)
        return total.astype(BF)

    def z_near(s):
        return (zl, zl + 1 - 2 * (zl % 2), zl + 2 - 4 * (zl // 2), 3 - zl)[s]

    def second_hop():
        arrived(a_in.at[pl.ds(0, n_dp - 1)], r_hop.at[0])
        arrived(tid_all.at[pl.ds(0, n_dp - 1)], r_hop.at[5])
        loads[1].wait()
        mine = a.at[f, pl.ds(pl.multiple_of(y * pr, pr), pr)]

        def send(j, s):
            dev = (j * 2 + zh, x * 8 + z_near(s) * 2 + c)
            remote(q_out.at[j], mine, s_hop.at[1], ra_z.at[s], dev).start()

        def hop2(k, _):
            j = (y + n_y // 2 + (k + 1) // 2 * (2 * (k % 2) - 1)) % n_y
            q_out[j] = choose(j * 2 + zh)
            for s in range(4):
                send(j, s)
            return 0

        lax.fori_loop(0, n_y - 1, hop2, 0)
        q_out[y] = choose(g)
        for s in (1, 2, 3):
            send(y, s)
        a[f, pl.ds(pl.multiple_of(y * pr, pr), pr)] = q_out[y]

    def b_start():
        loads[2].wait()
        arrived(b_in.at[pl.ds(0, n_dp - 1)], r_hop.at[4])
        bt_in[c, chip] = b_in[tenant]
        ref = bt_in.at[c, chip]

        def step(k, _):
            remote(ref, ref, s_hop.at[7], r_hop.at[7], chip_peer(k)).start()
            return 0

        lax.fori_loop(1, N_CHIP, step, 0)

    def b_hand():
        ref = bt_in.at[c]
        arrived(bt_in.at[c, pl.ds(0, N_CHIP - 1)], r_hop.at[7])
        remote(ref, ref, s_hop.at[8], r_hop.at[8], partner).start()

    def b_finish():
        arrived(bt_in.at[1 - c], r_hop.at[8])
        for k in range(N_CHIP):
            for core in (0, 1):
                row = (2 * k + core) * CB
                bt[row : row + CB] = bt_in[core, k]
        glow[...] = jnp.where(rank_live, scale * dot_nn(masked[...], bt[...]), 0.0).astype(BF)

    def a_slot(dx, s):
        return ((x + dx) % NX) * 8 + z_near(s) * 2 + c

    def a_other(dx, s):
        return a_slot(dx, s) + 1 - 2 * c

    def a_d2d(ref, sem):
        remote(ref, ref, sa_d2d, sem, partner).start()

    def a_block_wait(s):
        block = a_slot(0, s)
        ref = a.at[block]
        if s:
            arrived(ref, ra_z.at[s])
        else:
            arrived(a.at[f, pl.ds(0, (n_y - 1) * pr)], ra_z.at[0])
        remote(ref, ref, sa_ici, ra_x.at[s, 0], x_up).start()
        remote(ref, ref, sa_ici, ra_x.at[s, 1], x_dn).start()
        a_d2d(ref, ra_dz.at[s])

    def a_x_wait(s):
        dn = a.at[a_slot(3, s)]
        arrived(dn, ra_x.at[s, 0])
        part = a.at[a_slot(3, s), pl.ds(0, AH)]
        remote(part, part, sa_ici, ra_x.at[s, 2], x_up).start()
        a_d2d(dn, ra_dx.at[s, 0])
        up = a.at[a_slot(1, s)]
        arrived(up, ra_x.at[s, 1])
        part = a.at[a_slot(1, s), pl.ds(AH, AH)]
        remote(part, part, sa_ici, ra_x.at[s, 3], x_dn).start()
        a_d2d(up, ra_dx.at[s, 1])

    def a_x_last(s):
        lo = a.at[a_slot(2, s), pl.ds(0, AH)]
        arrived(lo, ra_x.at[s, 2])
        a_d2d(lo, ra_dx.at[s, 2])
        hi = a.at[a_slot(2, s), pl.ds(AH, AH)]
        arrived(hi, ra_x.at[s, 3])
        a_d2d(hi, ra_dx.at[s, 3])

    def a_other_z(s):
        arrived(a.at[a_other(0, s)], ra_dz.at[s])

    def a_other_x(s):
        arrived(a.at[a_other(3, s)], ra_dx.at[s, 0])
        arrived(a.at[a_other(1, s)], ra_dx.at[s, 1])

    def a_other_last(s):
        arrived(a.at[a_other(2, s), pl.ds(0, AH)], ra_dx.at[s, 2])
        arrived(a.at[a_other(2, s), pl.ds(AH, AH)], ra_dx.at[s, 3])

    def low_of(dx):
        def step(k, _):
            b = (x + dx) % NX * 2 * NZL + k
            low_acc[...] += dot_nn(tok[:, pl.ds(pl.multiple_of(b * RW, RW), RW)], a[b])
            return 0

        lax.fori_loop(0, 2 * NZL, step, 0)

    def cols(p):
        return pl.ds(pl.multiple_of(p * 2 * RW, 2 * RW), 2 * RW)

    def forward(p):
        proj_acc[...] += dot_nn(tok[:, cols(p)], w[cols(p)])

    def backward(p):
        base = dot_nt(masked[...], w[cols(p)])
        low_part = jnp.concatenate([dot_nt(glow[...], a[2 * p + k]) for k in (0, 1)], axis=1)
        gx_ref[:, cols(p)] = (base + low_part).astype(BF)

    def over(pairs, body):
        code_x = sum((dx % 4) * 4**i for i, (dx, dz) in enumerate(pairs))
        code_z = sum((dz % 4) * 4**i for i, (dx, dz) in enumerate(pairs))

        def step(_, carry):
            cx, cz = carry
            body(((x + cx % 4) % NX) * 4 + (zl + cz % 4) % NZL)
            return cx // 4, cz // 4

        lax.fori_loop(0, len(pairs), step, (jnp.int32(code_x), jnp.int32(code_z)))

    def others(pairs):
        for dx, dz in pairs:
            w_other(dx, dz)

    def both(p):
        forward(p)
        backward(p)

    loads[0].wait()
    first_start()
    hop1_b()
    second_start(0)
    prepare()
    first_wait(3)
    first_wait(1)
    second_start(3)
    second_start(1)
    second_hop()
    first_wait(2)
    second_start(2)
    second_wait(0)
    b_start()
    loads[4].wait()
    for s in range(4):
        a_block_wait(s)
    second_wait(3)
    for s in range(4):
        a_other_z(s)
    low_of(0)
    for s in range(4):
        a_x_wait(s)
    for s in range(4):
        a_other_x(s)
    low_of(1)
    low_of(3)
    b_hand()
    for s in range(4):
        a_x_last(s)
    for s in range(4):
        a_other_last(s)
    low_of(2)

    low = jnp.where(rank_live, low_acc[...], 0.0).astype(BF)
    terms = lax.dot_general(masked[...], low, (((0,), (0,)), ((), ())), preferred_element_type=F32) * scale
    terms = terms.reshape(N_CHIP, 2, CB, R)
    rs_out[0] = terms[:, 0]
    rs_out[1] = terms[:, 1]
    core_sum = remote(rs_out.at[1 - c], rs_mid, s_hop.at[2], r_hop.at[2], partner)
    core_sum.start()
    core_sum.wait_recv()
    rs_mid[...] = rs_mid[...] + rs_out[c]
    rs_in[chip] = rs_mid[chip]

    def scatter(k, _):
        remote(rs_mid.at[(chip + k) % N_CHIP], rs_in.at[chip], s_hop.at[6], r_hop.at[6], chip_peer(k)).start()
        return 0

    lax.fori_loop(1, N_CHIP, scatter, 0)

    b_finish()
    proj_acc[...] += scale_wide * dot_nt(low, bt[...])
    second_wait(1)
    second_wait(2)
    near = [(1, 0), (3, 0), (0, 1), (0, 3)]
    sides(near)
    others([(0, 0)] + near)
    over([(0, 0)] + near, both)

    arrived(rs_in.at[pl.ds(0, N_CHIP - 1)], r_hop.at[6])
    total = rs_in[0]
    for k in range(1, N_CHIP):
        total = total + rs_in[k]
    dp_out[...] = total
    dp_in[g] = total

    for peer in dp_peers:
        remote(dp_out, dp_in.at[g], s_hop.at[3], r_hop.at[3], peer).start()

    last_wait(0)
    last_wait(3)
    last_wait(1)
    middle = [(1, 1), (1, 3), (3, 1), (3, 3)]
    sides(middle)
    others(middle)
    over(middle, both)
    last_wait(2)
    late = [(2, 0), (0, 2), (2, 1), (1, 2), (2, 3), (3, 2), (2, 2)]
    sides(late)
    others(late)
    over(late, both)
    proj_ref[...] = jnp.where(row_live, proj_acc[...], 0.0).astype(BF)

    arrived(dp_in.at[pl.ds(0, n_dp - 1)], r_hop.at[3])
    total = jnp.zeros((CB, R), F32)
    for k in range(n_dp):
        total = total + jnp.where(jnp.broadcast_to(tid_all[k], (CB, R)) == g, dp_in[k], 0.0)
    gup_ref[...] = total

    sent(w.at[pl.ds(0, 15 * RW)], sw_ici)
    sent(w.at[pl.ds(0, 16 * RW)], sw_d2d)
    sent(a.at[pl.ds(0, 12)], sa_ici)

    sent(a.at[pl.ds(0, 16)], sa_d2d)
    sent(a_in.at[pl.ds(0, n_dp - 1)], s_hop.at[0])
    sent(a.at[pl.ds(0, 3)], s_hop.at[1])
    sent(a.at[0, pl.ds(0, (n_y - 1) * pr)], s_hop.at[1])
    sent(bt_in.at[0, pl.ds(0, N_CHIP - 1)], s_hop.at[7])
    sent(bt_in.at[0], s_hop.at[8])
    core_sum.wait_send()
    sent(dp_in.at[pl.ds(0, n_dp - 1)], s_hop.at[3])
    sent(b_in.at[pl.ds(0, n_dp - 1)], s_hop.at[4])
    sent(tid_all.at[pl.ds(0, n_dp - 1)], s_hop.at[5])
    sent(rs_in.at[pl.ds(0, N_CHIP - 1)], s_hop.at[6])


def per_device(
    tokens, grad_out, base_weight, frozen_down, trained_up, tenant_per_group, lengths, ranks
):
    n_dp = ranks.shape[0]
    pr = RW // (n_dp // 2)
    hbm = pl.BlockSpec(memory_space=pltpu.HBM)
    smem = pl.BlockSpec(memory_space=pltpu.SMEM)
    vmem = pl.BlockSpec(memory_space=pltpu.VMEM)
    dma = pltpu.SemaphoreType.DMA
    projected, grad_x, up = pl.pallas_call(
        functools.partial(kernel, n_dp),
        out_shape=(
            jax.ShapeDtypeStruct((TOK, VW), BF),
            jax.ShapeDtypeStruct((TOK, N_FSDP * RW), BF),
            jax.ShapeDtypeStruct((CB, R), F32),
        ),
        in_specs=[hbm] * 5 + [smem] * 3,
        out_specs=(vmem, vmem, vmem),
        scratch_shapes=[
            pltpu.VMEM((TOK, N_FSDP * RW), BF),
            pltpu.VMEM((TOK, VW), BF),
            pltpu.VMEM((TOK, R), BF),
            pltpu.VMEM((N_FSDP * RW, VW), BF),
            pltpu.VMEM((N_FSDP, RW, R), BF),
            pltpu.VMEM((n_dp, 1, R), jnp.int32),
            pltpu.VMEM((n_dp, pr, R), BF),
            pltpu.VMEM((n_dp, CB, R), BF),
            pltpu.VMEM((n_dp // 2, pr, R), BF),
            pltpu.VMEM((2, N_CHIP, CB, R), BF),
            pltpu.VMEM((VW, R), BF),
            pltpu.VMEM((2, N_CHIP, CB, R), F32),
            pltpu.VMEM((N_CHIP, CB, R), F32),
            pltpu.VMEM((N_CHIP, CB, R), F32),
            pltpu.VMEM((CB, R), F32),
            pltpu.VMEM((n_dp, CB, R), F32),
            pltpu.VMEM((TOK, VW), F32),
            pltpu.VMEM((TOK, R), F32),
            dma((5,)),
            dma,
            dma,
            dma,
            dma,
            dma((9,)),
            dma((3, 16, 2)),
            dma((3, 16, 2)),
            dma((4,)),
            dma((4, 4)),
            dma((4,)),
            dma((4, 4)),
            dma((9,)),
        ],
        compiler_params=pltpu.CompilerParams(
            collective_id=0, has_side_effects=True, vmem_limit_bytes=40 * 1024 * 1024
        ),
        cost_estimate=pl.CostEstimate(
            flops=2 * 2 * TOK * N_FSDP * RW * (VW + R), bytes_accessed=5 * 1024 * 1024, transcendentals=0
        ),
        name="gather_and_multiply",
    )(
        *[pltpu.with_memory_space_constraint(v, pltpu.HBM) for v in (tokens, grad_out, base_weight, frozen_down[0], jnp.swapaxes(trained_up[0], 0, 1))],
        tenant_per_group, lengths, ranks,
    )
    return projected, grad_x, jnp.swapaxes(up, 0, 1)[None]


def solution(mesh):
    placed = (
        P(("dp", "fsdp"), None),
        P(("dp", "fsdp"), None),
        P("fsdp", None),
        P("dp", "fsdp", None),
        P("dp", None, "fsdp"),
        P("dp"),
        P("dp", "fsdp"),
        P(),
    )
    return jax.shard_map(
        per_device,
        mesh=mesh,
        in_specs=placed,
        out_specs=(P(("dp", "fsdp"), None), P(("dp", "fsdp"), None), P("dp", None, "fsdp")),
        check_vma=False,
    )
```

```python
import functools

import jax
import jax.numpy as jnp
from jax import lax
from jax.experimental import pallas as pl
from jax.experimental.pallas import tpu as pltpu
from jax.sharding import PartitionSpec as P

adapter_alpha_factor = 2.0

MESH = pl.DeviceIdType.MESH
BF, F32 = jnp.bfloat16, jnp.float32

NX = 4
NZL = 4
NZ = 8
N_FSDP = 32
RW = 256
VW = 512
R = 128
TOK = 128
N_CHIP = N_FSDP // 2
CB = VW // N_FSDP
AH = RW // 2
SIDE = 96


def dot_nn(a, b):
    return lax.dot_general(a, b, (((1,), (0,)), ((), ())), preferred_element_type=F32)


def dot_nt(a, b):
    return lax.dot_general(a, b, (((1,), (1,)), ((), ())), preferred_element_type=F32)


def kernel(
    n_dp, tok_hbm, grad_hbm, w_hbm, a_hbm, bt_hbm, tid_s, len_s, rank_hbm,
    proj_ref, gx_ref, gup_ref,
    rank_s, tok, masked, glow, w, a, tid_all, a_in, b_in, q_out, bt_in, bt, rs_out, rs_mid, rs_in, dp_out, dp_in,
    proj_acc, low_acc,
    load_sem, sw_ici, sw_d2d, sa_ici, sa_d2d, s_hop, rw_ici, rw_d2d, ra_z, ra_x, ra_dz, ra_dx, r_hop,
):
    n_y = n_dp // 2
    pr = RW // n_y
    g = lax.axis_index("dp")
    f = lax.axis_index("fsdp")
    y, zh = g // 2, g % 2
    x, zl, c = f // 8, (f // 2) % 4, f % 2
    z = zh * NZL + zl

    def at(dx, dz):
        xx, zz = (x + dx) % NX, (z + dz) % NZ
        return (y * 2 + zz // NZL, xx * 8 + (zz % NZL) * 2 + c)

    partner = (g, f + 1 - 2 * c)
    x_up, x_dn = at(1, 0), at(NX - 1, 0)
    z_up, z_dn = at(0, 1), at(0, NZ - 1)
    y_up, y_dn = ((y + 1) % n_y * 2 + zh, f), ((y + n_y - 1) % n_y * 2 + zh, f)

    loads = [
        pltpu.make_async_copy(w_hbm, w.at[pl.ds(pl.multiple_of(f * RW, RW), RW)], load_sem.at[0]),
        pltpu.make_async_copy(a_hbm.at[pl.ds(pl.multiple_of(y * pr, pr), pr)], a_in.at[g], load_sem.at[1]),
        pltpu.make_async_copy(bt_hbm, b_in.at[g], load_sem.at[2]),
        pltpu.make_async_copy(grad_hbm, masked, load_sem.at[3]),
        pltpu.make_async_copy(tok_hbm, tok, load_sem.at[4]),
    ]

    rank_load = pltpu.make_async_copy(rank_hbm, rank_s, load_sem.at[5])
    rank_load.start()

    by_distance = sorted(range(n_y), key=lambda d: -min(d, n_y - d))
    dp_peers = [((y + d) % n_y * 2 + (zh + e) % 2, f) for e in (1, 0) for d in by_distance if d or e]
    chip = f // 2

    def chip_peer(k):
        return (g, (chip + k) % N_CHIP * 2 + c)

    barrier = pltpu.get_barrier_semaphore()

    def greet(dev):
        pl.semaphore_signal(barrier, inc=1, device_id=dev, device_id_type=MESH)

    for peer in dp_peers:
        greet(peer)

    def greet_chips(k, _):
        greet(chip_peer(k))
        return 0

    lax.fori_loop(1, N_CHIP, greet_chips, 0)
    greet(z_up)
    greet(z_dn)
    greet(partner)
    for load in loads:
        load.start()
    tenant = tid_s[0]
    tid_all[g] = jnp.full((1, R), tenant, jnp.int32)

    def remote(src, dst, send, recv, dev):
        return pltpu.make_async_remote_copy(
            src_ref=src, dst_ref=dst, send_sem=send, recv_sem=recv, device_id=dev, device_id_type=MESH
        )

    def arrived(ref, sem):
        remote(ref, ref, s_hop.at[0], sem, partner).wait_recv()

    def sent(ref, sem):
        remote(ref, ref, sem, r_hop.at[0], partner).wait_send()

    pl.semaphore_wait(barrier, n_dp - 1 + N_CHIP - 1 + 3)

    for j, _ in dp_peers:
        rows = a_hbm.at[pl.ds(pl.multiple_of(j // 2 * pr, pr), pr)]
        remote(rows, a_in.at[g], s_hop.at[0], r_hop.at[0], (j, f)).start()
        remote(tid_all.at[g], tid_all.at[g], s_hop.at[5], r_hop.at[5], (j, f)).start()

    def hop1_b():
        remote(bt_hbm, b_in.at[g], s_hop.at[4], r_hop.at[4], (y * 2 + 1 - zh, f)).start()

    def hop2_b():
        loads[2].wait()
        arrived(b_in.at[g], r_hop.at[4])
        pair = b_in.at[pl.ds(y * 2, 2)]
        for d in range(1, n_y):
            remote(pair, pair, s_hop.at[4], r_hop.at[9], ((y + d) % n_y * 2 + zh, f)).start()

    def prepare():
        loads[3].wait()
        masked[...] = jnp.where(row_live, masked[...].astype(F32), 0.0).astype(BF)
        proj_acc[...] = jnp.zeros_like(proj_acc)
        low_acc[...] = jnp.zeros_like(low_acc)

    rank_load.wait()
    rank = rank_s[tenant]
    scale = adapter_alpha_factor / jnp.sqrt(jnp.full((1, R), rank, jnp.int32).astype(F32))
    scale_wide = adapter_alpha_factor / jnp.sqrt(jnp.full((1, VW), rank, jnp.int32).astype(F32))
    rank_live = lax.broadcasted_iota(jnp.int32, (TOK, R), 1) < rank
    row_live = lax.broadcasted_iota(jnp.int32, (TOK, VW), 0) < len_s[0, 0]

    def place(dx, dz):
        return ((x + dx) % NX) * 8 + ((zl + dz) % NZL) * 2 + c

    def rows_at(where, lo, first, last):
        return w.at[pl.ds(pl.multiple_of(where * RW + lo + first, 16), last - first)]

    def w_rows(dx, dz, *span):
        return rows_at(place(dx, dz), *span)

    odd = y % 2
    low_row = (odd * (RW - SIDE), SIDE, (1 - odd) * (RW - SIDE))
    size = (SIDE, RW - 2 * SIDE, SIDE)
    half = (48, 32, 0)

    def span(stream, part):
        lo = low_row[stream]
        ends = {"all": (0, size[stream]), "lo": (0, half[stream]), "hi": (half[stream], size[stream])}[part]
        return lo, ends[0], ends[1]

    def slot(dx, dz):
        return (dx % 4) * 4 + dz % 4

    def w_send(stream, dx, dz, part, axis, step):
        ref = w_rows(dx, dz, *span(stream, part))
        if axis == "x":
            dev = x_up if step == 1 else x_dn
            there = slot(dx - step, dz)
        else:
            dev = z_up if step == 1 else z_dn
            there = slot(dx, dz - step)
        remote(ref, ref, sw_ici, rw_ici.at[stream, there, int(part == "hi")], dev).start()

    def w_d2d(stream, dx, dz, part):
        ref = w_rows(dx, dz, *span(stream, part))
        remote(ref, ref, sw_d2d, rw_d2d.at[stream, slot(dx, dz), int(part == "hi")], partner).start()

    def w_wait(stream, dx, dz, part):
        arrived(w_rows(dx, dz, *span(stream, part)), rw_ici.at[stream, slot(dx, dz), int(part == "hi")])
        w_d2d(stream, dx, dz, part)

    def other_rows(dx, dz, *span):
        return rows_at(place(dx, dz) + 1 - 2 * c, *span)

    def w_other(dx, dz):
        if (dx, dz) == (0, 0):
            arrived(other_rows(0, 0, 0, 0, RW), rw_d2d.at[0, 0, 0])
            return
        for stream in (0, 1, 2):
            for part in parts_of(stream, dx, dz):
                arrived(other_rows(dx, dz, *span(stream, part)), rw_d2d.at[stream, slot(dx, dz), int(part == "hi")])

    def w_side(dx, dz):
        ref = w_rows(dx, dz, *span(0, "all"))
        dev = y_dn if (dx + dz) % 2 else y_up
        remote(ref, ref, sw_ici, rw_ici.at[2, slot(dx, dz), 0], dev).start()

    def w_side_wait(dx, dz):
        arrived(w_rows(dx, dz, *span(2, "all")), rw_ici.at[2, slot(dx, dz), 0])
        w_d2d(2, dx, dz, "all")

    def sides(pairs):
        for dx, dz in pairs:
            w_side_wait(dx, dz)

    def parts_of(stream, dx, dz):
        last = 0
        if stream == 0:
            last = dz if dz else dx
        elif stream == 1:
            last = dx if dx else dz
        return ("lo", "hi") if last == 2 else ("all",)

    def pick(stream, p, q):
        return (p, q) if stream == 0 else (q, p)

    axes = (("x", "z"), ("z", "x"))

    def first_start():
        for stream in (0, 1):
            for step in (1, -1):
                w_send(stream, 0, 0, "all", axes[stream][0], step)
        ref = w_rows(0, 0, 0, 0, RW)
        remote(ref, ref, sw_d2d, rw_d2d.at[0, 0, 0], partner).start()

    def second_start(p):
        for stream in (0, 1):
            for step in (1, -1):
                w_send(stream, *pick(stream, p, 0), "all", axes[stream][1], step)

    def first_wait(p):
        for stream in (0, 1):
            if p == 2:
                for part in ("lo", "hi"):
                    w_wait(stream, *pick(stream, p, 0), part)
                if stream == 0:
                    w_side(*pick(stream, p, 0))
            else:
                w_wait(stream, *pick(stream, p, 0), "all")
                if stream == 0:
                    w_side(*pick(stream, p, 0))
                if p == 3:
                    w_send(stream, *pick(stream, p, 0), "lo", axes[stream][0], 1)
                else:
                    w_send(stream, *pick(stream, p, 0), "hi", axes[stream][0], -1)

    def second_wait(p, streams=(0, 1)):
        for stream in streams:
            for q in (3, 1):
                w_wait(stream, *pick(stream, p, q), "all")
                if stream == 0:
                    w_side(*pick(stream, p, q))
                if q == 3:
                    w_send(stream, *pick(stream, p, q), "lo", axes[stream][1], 1)
                else:
                    w_send(stream, *pick(stream, p, q), "hi", axes[stream][1], -1)

    def last_wait(p, streams=(0, 1)):
        for stream in streams:
            for part in ("lo", "hi"):
                w_wait(stream, *pick(stream, p, 2), part)
            if stream == 0:
                w_side(*pick(stream, p, 2))

    def choose(k):
        tile = jnp.broadcast_to(tid_all[k], (pr, R))
        total = jnp.zeros((pr, R), F32)
        for u in range(n_dp):
            total = total + jnp.where(tile == u, a_in[u].astype(F32), 0.0)
        return total.astype(BF)

    def z_near(s):
        return (zl, zl + 1 - 2 * (zl % 2), zl + 2 - 4 * (zl // 2), 3 - zl)[s]

    def second_hop():
        arrived(a_in.at[pl.ds(0, n_dp - 1)], r_hop.at[0])
        arrived(tid_all.at[pl.ds(0, n_dp - 1)], r_hop.at[5])
        loads[1].wait()
        mine = a.at[f, pl.ds(pl.multiple_of(y * pr, pr), pr)]

        def send(j, s):
            dev = (j * 2 + zh, x * 8 + z_near(s) * 2 + c)
            remote(q_out.at[j], mine, s_hop.at[1], ra_z.at[s], dev).start()

        def hop2(k, _):
            j = (y + n_y // 2 + (k + 1) // 2 * (2 * (k % 2) - 1)) % n_y
            q_out[j] = choose(j * 2 + zh)
            for s in range(4):
                send(j, s)
            return 0

        lax.fori_loop(0, n_y - 1, hop2, 0)
        q_out[y] = choose(g)
        for s in (1, 2, 3):
            send(y, s)
        a[f, pl.ds(pl.multiple_of(y * pr, pr), pr)] = q_out[y]

    def b_start():
        arrived(b_in.at[pl.ds(0, n_dp - 2)], r_hop.at[9])
        bt_in[c, chip] = b_in[tenant]
        ref = bt_in.at[c, chip]

        def step(k, _):
            remote(ref, ref, s_hop.at[7], r_hop.at[7], chip_peer(k)).start()
            return 0

        lax.fori_loop(1, N_CHIP, step, 0)

    def b_hand():
        ref = bt_in.at[c]
        arrived(bt_in.at[c, pl.ds(0, N_CHIP - 1)], r_hop.at[7])
        remote(ref, ref, s_hop.at[8], r_hop.at[8], partner).start()

    def b_finish():
        arrived(bt_in.at[1 - c], r_hop.at[8])
        for k in range(N_CHIP):
            for core in (0, 1):
                row = (2 * k + core) * CB
                bt[row : row + CB] = bt_in[core, k]
        glow[...] = jnp.where(rank_live, scale * dot_nn(masked[...], bt[...]), 0.0).astype(BF)

    def a_slot(dx, s):
        return ((x + dx) % NX) * 8 + z_near(s) * 2 + c

    def a_other(dx, s):
        return a_slot(dx, s) + 1 - 2 * c

    def a_d2d(ref, sem):
        remote(ref, ref, sa_d2d, sem, partner).start()

    def a_block_wait(s):
        block = a_slot(0, s)
        ref = a.at[block]
        if s:
            arrived(ref, ra_z.at[s])
        else:
            arrived(a.at[f, pl.ds(0, (n_y - 1) * pr)], ra_z.at[0])
        remote(ref, ref, sa_ici, ra_x.at[s, 0], x_up).start()
        remote(ref, ref, sa_ici, ra_x.at[s, 1], x_dn).start()
        a_d2d(ref, ra_dz.at[s])

    def a_x_wait(s):
        dn = a.at[a_slot(3, s)]
        arrived(dn, ra_x.at[s, 0])
        part = a.at[a_slot(3, s), pl.ds(0, AH)]
        remote(part, part, sa_ici, ra_x.at[s, 2], x_up).start()
        a_d2d(dn, ra_dx.at[s, 0])
        up = a.at[a_slot(1, s)]
        arrived(up, ra_x.at[s, 1])
        part = a.at[a_slot(1, s), pl.ds(AH, AH)]
        remote(part, part, sa_ici, ra_x.at[s, 3], x_dn).start()
        a_d2d(up, ra_dx.at[s, 1])

    def a_x_last(s):
        lo = a.at[a_slot(2, s), pl.ds(0, AH)]
        arrived(lo, ra_x.at[s, 2])
        a_d2d(lo, ra_dx.at[s, 2])
        hi = a.at[a_slot(2, s), pl.ds(AH, AH)]
        arrived(hi, ra_x.at[s, 3])
        a_d2d(hi, ra_dx.at[s, 3])

    def a_other_z(s):
        arrived(a.at[a_other(0, s)], ra_dz.at[s])

    def a_other_x(s):
        arrived(a.at[a_other(3, s)], ra_dx.at[s, 0])
        arrived(a.at[a_other(1, s)], ra_dx.at[s, 1])

    def a_other_last(s):
        arrived(a.at[a_other(2, s), pl.ds(0, AH)], ra_dx.at[s, 2])
        arrived(a.at[a_other(2, s), pl.ds(AH, AH)], ra_dx.at[s, 3])

    def low_of(dx):
        def step(k, _):
            b = (x + dx) % NX * 2 * NZL + k
            low_acc[...] += dot_nn(tok[:, pl.ds(pl.multiple_of(b * RW, RW), RW)], a[b])
            return 0

        lax.fori_loop(0, 2 * NZL, step, 0)

    def cols(p):
        return pl.ds(pl.multiple_of(p * 2 * RW, 2 * RW), 2 * RW)

    def forward(p):
        proj_acc[...] += dot_nn(tok[:, cols(p)], w[cols(p)])

    def backward(p):
        base = dot_nt(masked[...], w[cols(p)])
        low_part = jnp.concatenate([dot_nt(glow[...], a[2 * p + k]) for k in (0, 1)], axis=1)
        gx_ref[:, cols(p)] = (base + low_part).astype(BF)

    def over(pairs, body):
        code_x = sum((dx % 4) * 4**i for i, (dx, dz) in enumerate(pairs))
        code_z = sum((dz % 4) * 4**i for i, (dx, dz) in enumerate(pairs))

        def step(_, carry):
            cx, cz = carry
            body(((x + cx % 4) % NX) * 4 + (zl + cz % 4) % NZL)
            return cx // 4, cz // 4

        lax.fori_loop(0, len(pairs), step, (jnp.int32(code_x), jnp.int32(code_z)))

    def others(pairs):
        for dx, dz in pairs:
            w_other(dx, dz)

    def both(p):
        forward(p)
        backward(p)

    loads[0].wait()
    first_start()
    hop1_b()
    second_start(0)
    prepare()
    second_hop()
    first_wait(3)
    first_wait(1)
    second_start(3)
    second_start(1)
    hop2_b()
    first_wait(2)
    second_start(2)
    second_wait(0)
    b_start()
    loads[4].wait()
    for s in range(4):
        a_block_wait(s)
    second_wait(3, (0,))
    second_wait(1, (0,))
    for s in range(4):
        a_other_z(s)
    low_of(0)
    for s in range(4):
        a_x_wait(s)
    second_wait(2, (0,))
    second_wait(3, (1,))
    for s in range(4):
        a_other_x(s)
    low_of(1)
    low_of(3)
    second_wait(1, (1,))
    b_hand()
    for s in range(4):
        a_x_last(s)
    for s in range(4):
        a_other_last(s)
    low_of(2)

    low = jnp.where(rank_live, low_acc[...], 0.0).astype(BF)
    terms = lax.dot_general(masked[...], low, (((0,), (0,)), ((), ())), preferred_element_type=F32) * scale
    terms = terms.reshape(N_CHIP, 2, CB, R)
    rs_out[0] = terms[:, 0]
    rs_out[1] = terms[:, 1]
    core_sum = remote(rs_out.at[1 - c], rs_mid, s_hop.at[2], r_hop.at[2], partner)
    core_sum.start()
    core_sum.wait_recv()
    rs_mid[...] = rs_mid[...] + rs_out[c]
    rs_in[chip] = rs_mid[chip]

    def scatter(k, _):
        remote(rs_mid.at[(chip + k) % N_CHIP], rs_in.at[chip], s_hop.at[6], r_hop.at[6], chip_peer(k)).start()
        return 0

    lax.fori_loop(1, N_CHIP, scatter, 0)

    b_finish()
    proj_acc[...] += scale_wide * dot_nt(low, bt[...])
    second_wait(2, (1,))
    last_wait(0, (0,))
    last_wait(3, (0,))
    last_wait(1, (0,))
    last_wait(2, (0,))
    near = [(1, 0), (3, 0), (0, 1), (0, 3)]
    sides(near)
    others([(0, 0)] + near)
    over([(0, 0)] + near, both)
    last_wait(0, (1,))
    last_wait(3, (1,))

    arrived(rs_in.at[pl.ds(0, N_CHIP - 1)], r_hop.at[6])
    total = rs_in[0]
    for k in range(1, N_CHIP):
        total = total + rs_in[k]
    dp_out[...] = total
    dp_in[g] = total

    for peer in dp_peers:
        remote(dp_out, dp_in.at[g], s_hop.at[3], r_hop.at[3], peer).start()

    def finish(pairs):
        sides(pairs)
        others(pairs)
        over(pairs, both)

    finish([(1, 1), (1, 3), (3, 1), (3, 3)])
    last_wait(1, (1,))
    finish([(2, 0), (0, 2)])
    last_wait(2, (1,))
    finish([(2, 3), (3, 2), (2, 1), (1, 2)])
    finish([(2, 2)])
    proj_ref[...] = jnp.where(row_live, proj_acc[...], 0.0).astype(BF)

    arrived(dp_in.at[pl.ds(0, n_dp - 1)], r_hop.at[3])
    total = jnp.zeros((CB, R), F32)
    for k in range(n_dp):
        total = total + jnp.where(jnp.broadcast_to(tid_all[k], (CB, R)) == g, dp_in[k], 0.0)
    gup_ref[...] = total

    sent(w.at[pl.ds(0, 15 * RW)], sw_ici)
    sent(w.at[pl.ds(0, 16 * RW)], sw_d2d)
    sent(a.at[pl.ds(0, 12)], sa_ici)

    sent(a.at[pl.ds(0, 16)], sa_d2d)
    sent(a_in.at[pl.ds(0, n_dp - 1)], s_hop.at[0])
    sent(a.at[pl.ds(0, 3)], s_hop.at[1])
    sent(a.at[0, pl.ds(0, (n_y - 1) * pr)], s_hop.at[1])
    sent(bt_in.at[0, pl.ds(0, N_CHIP - 1)], s_hop.at[7])
    sent(bt_in.at[0], s_hop.at[8])
    core_sum.wait_send()
    sent(dp_in.at[pl.ds(0, n_dp - 1)], s_hop.at[3])
    sent(b_in.at[pl.ds(0, n_dp - 1)], s_hop.at[4])
    sent(tid_all.at[pl.ds(0, n_dp - 1)], s_hop.at[5])
    sent(rs_in.at[pl.ds(0, N_CHIP - 1)], s_hop.at[6])


def per_device(
    tokens, grad_out, base_weight, frozen_down, trained_up, tenant_per_group, lengths, ranks
):
    n_dp = ranks.shape[0]
    pr = RW // (n_dp // 2)
    hbm = pl.BlockSpec(memory_space=pltpu.HBM)
    smem = pl.BlockSpec(memory_space=pltpu.SMEM)
    vmem = pl.BlockSpec(memory_space=pltpu.VMEM)
    dma = pltpu.SemaphoreType.DMA
    projected, grad_x, up = pl.pallas_call(
        functools.partial(kernel, n_dp),
        out_shape=(
            jax.ShapeDtypeStruct((TOK, VW), BF),
            jax.ShapeDtypeStruct((TOK, N_FSDP * RW), BF),
            jax.ShapeDtypeStruct((CB, R), F32),
        ),
        in_specs=[hbm] * 5 + [smem, smem, hbm],
        out_specs=(vmem, vmem, vmem),
        scratch_shapes=[
            pltpu.SMEM((n_dp,), jnp.int32),
            pltpu.VMEM((TOK, N_FSDP * RW), BF),
            pltpu.VMEM((TOK, VW), BF),
            pltpu.VMEM((TOK, R), BF),
            pltpu.VMEM((N_FSDP * RW, VW), BF),
            pltpu.VMEM((N_FSDP, RW, R), BF),
            pltpu.VMEM((n_dp, 1, R), jnp.int32),
            pltpu.VMEM((n_dp, pr, R), BF),
            pltpu.VMEM((n_dp, CB, R), BF),
            pltpu.VMEM((n_dp // 2, pr, R), BF),
            pltpu.VMEM((2, N_CHIP, CB, R), BF),
            pltpu.VMEM((VW, R), BF),
            pltpu.VMEM((2, N_CHIP, CB, R), F32),
            pltpu.VMEM((N_CHIP, CB, R), F32),
            pltpu.VMEM((N_CHIP, CB, R), F32),
            pltpu.VMEM((CB, R), F32),
            pltpu.VMEM((n_dp, CB, R), F32),
            pltpu.VMEM((TOK, VW), F32),
            pltpu.VMEM((TOK, R), F32),
            dma((6,)),
            dma,
            dma,
            dma,
            dma,
            dma((10,)),
            dma((3, 16, 2)),
            dma((3, 16, 2)),
            dma((4,)),
            dma((4, 4)),
            dma((4,)),
            dma((4, 4)),
            dma((10,)),
        ],
        compiler_params=pltpu.CompilerParams(
            collective_id=0, has_side_effects=True, vmem_limit_bytes=40 * 1024 * 1024
        ),
        cost_estimate=pl.CostEstimate(
            flops=2 * 2 * TOK * N_FSDP * RW * (VW + R), bytes_accessed=5 * 1024 * 1024, transcendentals=0
        ),
        name="gather_and_multiply",
    )(
        *[
            pltpu.with_memory_space_constraint(v, pltpu.HBM)
            for v in (
                tokens, grad_out, base_weight, frozen_down[0], jnp.swapaxes(trained_up[0], 0, 1)
            )
        ],
        tenant_per_group, lengths, pltpu.with_memory_space_constraint(ranks, pltpu.HBM),
    )
    return projected, grad_x, jnp.swapaxes(up, 0, 1)[None]


def solution(mesh):
    placed = (
        P(("dp", "fsdp"), None),
        P(("dp", "fsdp"), None),
        P("fsdp", None),
        P("dp", "fsdp", None),
        P("dp", None, "fsdp"),
        P("dp"),
        P("dp", "fsdp"),
        P(),
    )
    return jax.shard_map(
        per_device,
        mesh=mesh,
        in_specs=placed,
        out_specs=(P(("dp", "fsdp"), None), P(("dp", "fsdp"), None), P("dp", None, "fsdp")),
        check_vma=False,
    )
```

```python
import functools

import jax
import jax.numpy as jnp
from jax import lax
from jax.experimental import pallas as pl
from jax.experimental.pallas import tpu as pltpu
from jax.sharding import PartitionSpec as P

adapter_alpha_factor = 2.0

MESH = pl.DeviceIdType.MESH
BF, F32 = jnp.bfloat16, jnp.float32

NX = 4
NZL = 4
NZ = 8
N_FSDP = 32
RW = 256
VW = 512
R = 128
TOK = 128
N_CHIP = N_FSDP // 2
CB = VW // N_FSDP
AH = RW // 2
SIDE = 96


def dot_nn(a, b):
    return lax.dot_general(a, b, (((1,), (0,)), ((), ())), preferred_element_type=F32)


def dot_nt(a, b):
    return lax.dot_general(a, b, (((1,), (1,)), ((), ())), preferred_element_type=F32)


def kernel(
    n_dp, tok_hbm, grad_hbm, w_hbm, a_hbm, bt_hbm, tid_s, len_s, rank_hbm,
    proj_ref, gx_ref, gup_ref,
    rank_s, tok, masked, glow, w, a, tid_all, a_in, b_in, q_out, bt_in, bt, rs_out, rs_mid, rs_in, dp_out, dp_in,
    proj_acc, low_acc,
    load_sem, sw_ici, sw_d2d, sa_ici, sa_d2d, s_hop, rw_ici, rw_d2d, ra_z, ra_x, ra_dz, ra_dx, r_hop,
):
    n_y = n_dp // 2
    pr = RW // n_y
    g = lax.axis_index("dp")
    f = lax.axis_index("fsdp")
    y, zh = g // 2, g % 2
    x, zl, c = f // 8, (f // 2) % 4, f % 2
    z = zh * NZL + zl

    def at(dx, dz):
        xx, zz = (x + dx) % NX, (z + dz) % NZ
        return (y * 2 + zz // NZL, xx * 8 + (zz % NZL) * 2 + c)

    partner = (g, f + 1 - 2 * c)
    x_up, x_dn = at(1, 0), at(NX - 1, 0)
    z_up, z_dn = at(0, 1), at(0, NZ - 1)
    y_up, y_dn = ((y + 1) % n_y * 2 + zh, f), ((y + n_y - 1) % n_y * 2 + zh, f)

    loads = [
        pltpu.make_async_copy(w_hbm, w.at[pl.ds(pl.multiple_of(f * RW, RW), RW)], load_sem.at[0]),
        pltpu.make_async_copy(a_hbm.at[pl.ds(pl.multiple_of(y * pr, pr), pr)], a_in.at[g], load_sem.at[1]),
        pltpu.make_async_copy(bt_hbm, b_in.at[g], load_sem.at[2]),
        pltpu.make_async_copy(grad_hbm, masked, load_sem.at[3]),
        pltpu.make_async_copy(tok_hbm, tok, load_sem.at[4]),
    ]

    rank_load = pltpu.make_async_copy(rank_hbm, rank_s, load_sem.at[5])
    rank_load.start()

    by_distance = sorted(range(n_y), key=lambda d: -min(d, n_y - d))
    dp_peers = [((y + d) % n_y * 2 + (zh + e) % 2, f) for e in (1, 0) for d in by_distance if d or e]
    chip = f // 2

    def chip_peer(k):
        return (g, (chip + k) % N_CHIP * 2 + c)

    barrier = pltpu.get_barrier_semaphore()

    def greet(dev):
        pl.semaphore_signal(barrier, inc=1, device_id=dev, device_id_type=MESH)

    for peer in dp_peers:
        greet(peer)

    def greet_chips(k, _):
        greet(chip_peer(k))
        return 0

    lax.fori_loop(1, N_CHIP, greet_chips, 0)
    greet(z_up)
    greet(z_dn)
    greet(partner)
    for load in loads:
        load.start()
    tenant = tid_s[0]
    tid_all[g] = jnp.full((1, R), tenant, jnp.int32)

    def remote(src, dst, send, recv, dev):
        return pltpu.make_async_remote_copy(
            src_ref=src, dst_ref=dst, send_sem=send, recv_sem=recv, device_id=dev, device_id_type=MESH
        )

    def arrived(ref, sem):
        remote(ref, ref, s_hop.at[0], sem, partner).wait_recv()

    def sent(ref, sem):
        remote(ref, ref, sem, r_hop.at[0], partner).wait_send()

    pl.semaphore_wait(barrier, n_dp - 1 + N_CHIP - 1 + 3)

    for j, _ in dp_peers:
        rows = a_hbm.at[pl.ds(pl.multiple_of(j // 2 * pr, pr), pr)]
        remote(rows, a_in.at[g], s_hop.at[0], r_hop.at[0], (j, f)).start()
        remote(tid_all.at[g], tid_all.at[g], s_hop.at[5], r_hop.at[5], (j, f)).start()

    def hop1_b():
        remote(bt_hbm, b_in.at[g], s_hop.at[4], r_hop.at[4], (y * 2 + 1 - zh, f)).start()

    def hop2_b():
        loads[2].wait()
        arrived(b_in.at[g], r_hop.at[4])
        pair = b_in.at[pl.ds(y * 2, 2)]
        for d in range(1, n_y):
            remote(pair, pair, s_hop.at[4], r_hop.at[9], ((y + d) % n_y * 2 + zh, f)).start()

    def prepare():
        loads[3].wait()
        masked[...] = jnp.where(row_live, masked[...].astype(F32), 0.0).astype(BF)
        proj_acc[...] = jnp.zeros_like(proj_acc)
        low_acc[...] = jnp.zeros_like(low_acc)

    rank_load.wait()
    rank = rank_s[tenant]
    scale = adapter_alpha_factor / jnp.sqrt(jnp.full((1, R), rank, jnp.int32).astype(F32))
    scale_wide = adapter_alpha_factor / jnp.sqrt(jnp.full((1, VW), rank, jnp.int32).astype(F32))
    rank_live = lax.broadcasted_iota(jnp.int32, (TOK, R), 1) < rank
    row_live = lax.broadcasted_iota(jnp.int32, (TOK, VW), 0) < len_s[0, 0]

    def place(dx, dz):
        return ((x + dx) % NX) * 8 + ((zl + dz) % NZL) * 2 + c

    def rows_at(where, lo, first, last):
        return w.at[pl.ds(pl.multiple_of(where * RW + lo + first, 16), last - first)]

    def w_rows(dx, dz, *span):
        return rows_at(place(dx, dz), *span)

    odd = y % 2
    low_row = (odd * (RW - SIDE), SIDE, (1 - odd) * (RW - SIDE))
    size = (SIDE, RW - 2 * SIDE, SIDE)
    half = (48, 32, 0)

    def span(stream, part):
        lo = low_row[stream]
        ends = {"all": (0, size[stream]), "lo": (0, half[stream]), "hi": (half[stream], size[stream])}[part]
        return lo, ends[0], ends[1]

    def slot(dx, dz):
        return (dx % 4) * 4 + dz % 4

    def w_send(stream, dx, dz, part, axis, step):
        ref = w_rows(dx, dz, *span(stream, part))
        if axis == "x":
            dev = x_up if step == 1 else x_dn
            there = slot(dx - step, dz)
        else:
            dev = z_up if step == 1 else z_dn
            there = slot(dx, dz - step)
        remote(ref, ref, sw_ici, rw_ici.at[stream, there, int(part == "hi")], dev).start()

    def w_d2d(stream, dx, dz, part):
        ref = w_rows(dx, dz, *span(stream, part))
        remote(ref, ref, sw_d2d, rw_d2d.at[stream, slot(dx, dz), int(part == "hi")], partner).start()

    def w_wait(stream, dx, dz, part):
        arrived(w_rows(dx, dz, *span(stream, part)), rw_ici.at[stream, slot(dx, dz), int(part == "hi")])
        w_d2d(stream, dx, dz, part)

    def other_rows(dx, dz, *span):
        return rows_at(place(dx, dz) + 1 - 2 * c, *span)

    def w_other(dx, dz):
        if (dx, dz) == (0, 0):
            arrived(other_rows(0, 0, 0, 0, RW), rw_d2d.at[0, 0, 0])
            return
        for stream in (0, 1, 2):
            for part in parts_of(stream, dx, dz):
                arrived(other_rows(dx, dz, *span(stream, part)), rw_d2d.at[stream, slot(dx, dz), int(part == "hi")])

    def w_side(dx, dz):
        ref = w_rows(dx, dz, *span(0, "all"))
        dev = y_dn if (dx + dz) % 2 else y_up
        remote(ref, ref, sw_ici, rw_ici.at[2, slot(dx, dz), 0], dev).start()

    def w_side_wait(dx, dz):
        arrived(w_rows(dx, dz, *span(2, "all")), rw_ici.at[2, slot(dx, dz), 0])
        w_d2d(2, dx, dz, "all")

    def sides(pairs):
        for dx, dz in pairs:
            w_side_wait(dx, dz)

    def parts_of(stream, dx, dz):
        last = 0
        if stream == 0:
            last = dz if dz else dx
        elif stream == 1:
            last = dx if dx else dz
        return ("lo", "hi") if last == 2 else ("all",)

    def pick(stream, p, q):
        return (p, q) if stream == 0 else (q, p)

    axes = (("x", "z"), ("z", "x"))

    def first_start():
        for stream in (0, 1):
            for step in (1, -1):
                w_send(stream, 0, 0, "all", axes[stream][0], step)
        ref = w_rows(0, 0, 0, 0, RW)
        remote(ref, ref, sw_d2d, rw_d2d.at[0, 0, 0], partner).start()

    def second_start(p):
        for stream in (0, 1):
            for step in (1, -1):
                w_send(stream, *pick(stream, p, 0), "all", axes[stream][1], step)

    def first_wait(p):
        for stream in (0, 1):
            if p == 2:
                for part in ("lo", "hi"):
                    w_wait(stream, *pick(stream, p, 0), part)
                if stream == 0:
                    w_side(*pick(stream, p, 0))
            else:
                w_wait(stream, *pick(stream, p, 0), "all")
                if stream == 0:
                    w_side(*pick(stream, p, 0))
                if p == 3:
                    w_send(stream, *pick(stream, p, 0), "lo", axes[stream][0], 1)
                else:
                    w_send(stream, *pick(stream, p, 0), "hi", axes[stream][0], -1)

    def second_wait(p, streams=(0, 1)):
        for stream in streams:
            for q in (3, 1):
                w_wait(stream, *pick(stream, p, q), "all")
                if stream == 0:
                    w_side(*pick(stream, p, q))
                if q == 3:
                    w_send(stream, *pick(stream, p, q), "lo", axes[stream][1], 1)
                else:
                    w_send(stream, *pick(stream, p, q), "hi", axes[stream][1], -1)

    def last_wait(p, streams=(0, 1)):
        for stream in streams:
            for part in ("lo", "hi"):
                w_wait(stream, *pick(stream, p, 2), part)
            if stream == 0:
                w_side(*pick(stream, p, 2))

    def choose(k):
        tile = jnp.broadcast_to(tid_all[k], (pr, R))
        total = jnp.zeros((pr, R), F32)
        for u in range(n_dp):
            total = total + jnp.where(tile == u, a_in[u].astype(F32), 0.0)
        return total.astype(BF)

    def z_near(s):
        return (zl, zl + 1 - 2 * (zl % 2), zl + 2 - 4 * (zl // 2), 3 - zl)[s]

    def second_hop():
        arrived(a_in.at[pl.ds(0, n_dp - 1)], r_hop.at[0])
        arrived(tid_all.at[pl.ds(0, n_dp - 1)], r_hop.at[5])
        loads[1].wait()
        mine = a.at[f, pl.ds(pl.multiple_of(y * pr, pr), pr)]

        def send(j, s):
            dev = (j * 2 + zh, x * 8 + z_near(s) * 2 + c)
            remote(q_out.at[j], mine, s_hop.at[1], ra_z.at[s], dev).start()

        def hop2(k, _):
            j = (y + n_y // 2 + (k + 1) // 2 * (2 * (k % 2) - 1)) % n_y
            q_out[j] = choose(j * 2 + zh)
            for s in range(4):
                send(j, s)
            return 0

        lax.fori_loop(0, n_y - 1, hop2, 0)
        q_out[y] = choose(g)
        for s in (1, 2, 3):
            send(y, s)
        a[f, pl.ds(pl.multiple_of(y * pr, pr), pr)] = q_out[y]

    def b_start():
        arrived(b_in.at[pl.ds(0, n_dp - 2)], r_hop.at[9])
        bt_in[c, chip] = b_in[tenant]
        ref = bt_in.at[c, chip]

        def step(k, _):
            remote(ref, ref, s_hop.at[7], r_hop.at[7], chip_peer(k)).start()
            return 0

        lax.fori_loop(1, N_CHIP, step, 0)

    def b_hand():
        ref = bt_in.at[c]
        arrived(bt_in.at[c, pl.ds(0, N_CHIP - 1)], r_hop.at[7])
        remote(ref, ref, s_hop.at[8], r_hop.at[8], partner).start()

    def b_finish():
        arrived(bt_in.at[1 - c], r_hop.at[8])
        for k in range(N_CHIP):
            for core in (0, 1):
                row = (2 * k + core) * CB
                bt[row : row + CB] = bt_in[core, k]
        glow[...] = jnp.where(rank_live, scale * dot_nn(masked[...], bt[...]), 0.0).astype(BF)

    def a_slot(dx, s):
        return ((x + dx) % NX) * 8 + z_near(s) * 2 + c

    def a_other(dx, s):
        return a_slot(dx, s) + 1 - 2 * c

    def a_d2d(ref, sem):
        remote(ref, ref, sa_d2d, sem, partner).start()

    def a_block_wait(s):
        block = a_slot(0, s)
        ref = a.at[block]
        if s:
            arrived(ref, ra_z.at[s])
        else:
            arrived(a.at[f, pl.ds(0, (n_y - 1) * pr)], ra_z.at[0])
        remote(ref, ref, sa_ici, ra_x.at[s, 0], x_up).start()
        remote(ref, ref, sa_ici, ra_x.at[s, 1], x_dn).start()
        a_d2d(ref, ra_dz.at[s])

    def a_x_wait(s):
        dn = a.at[a_slot(3, s)]
        arrived(dn, ra_x.at[s, 0])
        part = a.at[a_slot(3, s), pl.ds(0, AH)]
        remote(part, part, sa_ici, ra_x.at[s, 2], x_up).start()
        a_d2d(dn, ra_dx.at[s, 0])
        up = a.at[a_slot(1, s)]
        arrived(up, ra_x.at[s, 1])
        part = a.at[a_slot(1, s), pl.ds(AH, AH)]
        remote(part, part, sa_ici, ra_x.at[s, 3], x_dn).start()
        a_d2d(up, ra_dx.at[s, 1])

    def a_x_last(s):
        lo = a.at[a_slot(2, s), pl.ds(0, AH)]
        arrived(lo, ra_x.at[s, 2])
        a_d2d(lo, ra_dx.at[s, 2])
        hi = a.at[a_slot(2, s), pl.ds(AH, AH)]
        arrived(hi, ra_x.at[s, 3])
        a_d2d(hi, ra_dx.at[s, 3])

    def a_other_z(s):
        arrived(a.at[a_other(0, s)], ra_dz.at[s])

    def a_other_x(s):
        arrived(a.at[a_other(3, s)], ra_dx.at[s, 0])
        arrived(a.at[a_other(1, s)], ra_dx.at[s, 1])

    def a_other_last(s):
        arrived(a.at[a_other(2, s), pl.ds(0, AH)], ra_dx.at[s, 2])
        arrived(a.at[a_other(2, s), pl.ds(AH, AH)], ra_dx.at[s, 3])

    def low_of(dx):
        def step(k, _):
            b = (x + dx) % NX * 2 * NZL + k
            low_acc[...] += dot_nn(tok[:, pl.ds(pl.multiple_of(b * RW, RW), RW)], a[b])
            return 0

        lax.fori_loop(0, 2 * NZL, step, 0)

    def cols(p):
        return pl.ds(pl.multiple_of(p * 2 * RW, 2 * RW), 2 * RW)

    def forward(p):
        proj_acc[...] += dot_nn(tok[:, cols(p)], w[cols(p)])

    def backward(p):
        base = dot_nt(masked[...], w[cols(p)])
        low_part = jnp.concatenate([dot_nt(glow[...], a[2 * p + k]) for k in (0, 1)], axis=1)
        gx_ref[:, cols(p)] = (base + low_part).astype(BF)

    def over(pairs, body):
        code_x = sum((dx % 4) * 4**i for i, (dx, dz) in enumerate(pairs))
        code_z = sum((dz % 4) * 4**i for i, (dx, dz) in enumerate(pairs))

        def step(_, carry):
            cx, cz = carry
            body(((x + cx % 4) % NX) * 4 + (zl + cz % 4) % NZL)
            return cx // 4, cz // 4

        lax.fori_loop(0, len(pairs), step, (jnp.int32(code_x), jnp.int32(code_z)))

    def others(pairs):
        for dx, dz in pairs:
            w_other(dx, dz)

    def both(p):
        forward(p)
        backward(p)

    loads[0].wait()
    first_start()
    hop1_b()
    second_start(0)
    prepare()
    second_hop()
    first_wait(3)
    first_wait(1)
    second_start(3)
    second_start(1)
    hop2_b()
    first_wait(2)
    second_start(2)
    second_wait(0)
    b_start()
    loads[4].wait()
    for s in range(4):
        a_block_wait(s)
    second_wait(3, (0,))
    second_wait(1, (0,))
    for s in range(4):
        a_other_z(s)
    low_of(0)
    for s in range(4):
        a_x_wait(s)
    second_wait(2, (0,))
    second_wait(3, (1,))
    for s in range(4):
        a_other_x(s)
    low_of(1)
    low_of(3)
    second_wait(1, (1,))
    b_hand()
    for s in range(4):
        a_x_last(s)
    for s in range(4):
        a_other_last(s)
    low_of(2)

    low = jnp.where(rank_live, low_acc[...], 0.0).astype(BF)
    terms = lax.dot_general(masked[...], low, (((0,), (0,)), ((), ())), preferred_element_type=F32) * scale
    terms = terms.reshape(N_CHIP, 2, CB, R)
    rs_out[0] = terms[:, 0]
    rs_out[1] = terms[:, 1]
    core_sum = remote(rs_out.at[1 - c], rs_mid, s_hop.at[2], r_hop.at[2], partner)
    core_sum.start()
    core_sum.wait_recv()
    rs_mid[...] = rs_mid[...] + rs_out[c]
    rs_in[chip] = rs_mid[chip]

    def scatter(k, _):
        remote(rs_mid.at[(chip + k) % N_CHIP], rs_in.at[chip], s_hop.at[6], r_hop.at[6], chip_peer(k)).start()
        return 0

    lax.fori_loop(1, N_CHIP, scatter, 0)

    b_finish()
    proj_acc[...] += scale_wide * dot_nt(low, bt[...])
    second_wait(2, (1,))
    last_wait(0, (0,))
    last_wait(3, (0,))
    last_wait(1, (0,))
    last_wait(2, (0,))
    near = [(1, 0), (3, 0), (0, 1), (0, 3)]
    sides(near)
    others([(0, 0)] + near)
    over([(0, 0)] + near, both)
    last_wait(0, (1,))
    last_wait(3, (1,))

    arrived(rs_in.at[pl.ds(0, N_CHIP - 1)], r_hop.at[6])
    total = rs_in[0]
    for k in range(1, N_CHIP):
        total = total + rs_in[k]
    dp_out[...] = total
    dp_in[g] = total

    for peer in dp_peers:
        remote(dp_out, dp_in.at[g], s_hop.at[3], r_hop.at[3], peer).start()

    middle = [(1, 1), (1, 3), (3, 1), (3, 3)]
    late = [(2, 0), (0, 2), (2, 3), (3, 2), (2, 1), (1, 2), (2, 2)]
    sides(middle)
    last_wait(1, (1,))
    last_wait(2, (1,))
    sides(late)
    others(middle)
    over(middle, both)
    others(late)
    over(late, both)
    proj_ref[...] = jnp.where(row_live, proj_acc[...], 0.0).astype(BF)

    arrived(dp_in.at[pl.ds(0, n_dp - 1)], r_hop.at[3])
    total = jnp.zeros((CB, R), F32)
    for k in range(n_dp):
        total = total + jnp.where(jnp.broadcast_to(tid_all[k], (CB, R)) == g, dp_in[k], 0.0)
    gup_ref[...] = total

    sent(w.at[pl.ds(0, 15 * RW)], sw_ici)
    sent(w.at[pl.ds(0, 16 * RW)], sw_d2d)
    sent(a.at[pl.ds(0, 12)], sa_ici)

    sent(a.at[pl.ds(0, 16)], sa_d2d)
    sent(a_in.at[pl.ds(0, n_dp - 1)], s_hop.at[0])
    sent(a.at[pl.ds(0, 3)], s_hop.at[1])
    sent(a.at[0, pl.ds(0, (n_y - 1) * pr)], s_hop.at[1])
    sent(bt_in.at[0, pl.ds(0, N_CHIP - 1)], s_hop.at[7])
    sent(bt_in.at[0], s_hop.at[8])
    core_sum.wait_send()
    sent(dp_in.at[pl.ds(0, n_dp - 1)], s_hop.at[3])
    sent(b_in.at[pl.ds(0, n_dp - 1)], s_hop.at[4])
    sent(tid_all.at[pl.ds(0, n_dp - 1)], s_hop.at[5])
    sent(rs_in.at[pl.ds(0, N_CHIP - 1)], s_hop.at[6])


def per_device(
    tokens, grad_out, base_weight, frozen_down, trained_up, tenant_per_group, lengths, ranks
):
    n_dp = ranks.shape[0]
    pr = RW // (n_dp // 2)
    hbm = pl.BlockSpec(memory_space=pltpu.HBM)
    smem = pl.BlockSpec(memory_space=pltpu.SMEM)
    vmem = pl.BlockSpec(memory_space=pltpu.VMEM)
    dma = pltpu.SemaphoreType.DMA
    projected, grad_x, up = pl.pallas_call(
        functools.partial(kernel, n_dp),
        out_shape=(
            jax.ShapeDtypeStruct((TOK, VW), BF),
            jax.ShapeDtypeStruct((TOK, N_FSDP * RW), BF),
            jax.ShapeDtypeStruct((CB, R), F32),
        ),
        in_specs=[hbm] * 5 + [smem, smem, hbm],
        out_specs=(vmem, vmem, vmem),
        scratch_shapes=[
            pltpu.SMEM((n_dp,), jnp.int32),
            pltpu.VMEM((TOK, N_FSDP * RW), BF),
            pltpu.VMEM((TOK, VW), BF),
            pltpu.VMEM((TOK, R), BF),
            pltpu.VMEM((N_FSDP * RW, VW), BF),
            pltpu.VMEM((N_FSDP, RW, R), BF),
            pltpu.VMEM((n_dp, 1, R), jnp.int32),
            pltpu.VMEM((n_dp, pr, R), BF),
            pltpu.VMEM((n_dp, CB, R), BF),
            pltpu.VMEM((n_dp // 2, pr, R), BF),
            pltpu.VMEM((2, N_CHIP, CB, R), BF),
            pltpu.VMEM((VW, R), BF),
            pltpu.VMEM((2, N_CHIP, CB, R), F32),
            pltpu.VMEM((N_CHIP, CB, R), F32),
            pltpu.VMEM((N_CHIP, CB, R), F32),
            pltpu.VMEM((CB, R), F32),
            pltpu.VMEM((n_dp, CB, R), F32),
            pltpu.VMEM((TOK, VW), F32),
            pltpu.VMEM((TOK, R), F32),
            dma((6,)),
            dma,
            dma,
            dma,
            dma,
            dma((10,)),
            dma((3, 16, 2)),
            dma((3, 16, 2)),
            dma((4,)),
            dma((4, 4)),
            dma((4,)),
            dma((4, 4)),
            dma((10,)),
        ],
        compiler_params=pltpu.CompilerParams(
            collective_id=0, has_side_effects=True, vmem_limit_bytes=40 * 1024 * 1024
        ),
        cost_estimate=pl.CostEstimate(
            flops=2 * 2 * TOK * N_FSDP * RW * (VW + R), bytes_accessed=5 * 1024 * 1024, transcendentals=0
        ),
        name="gather_and_multiply",
    )(
        *[
            pltpu.with_memory_space_constraint(v, pltpu.HBM)
            for v in (
                tokens, grad_out, base_weight, frozen_down[0], jnp.swapaxes(trained_up[0], 0, 1)
            )
        ],
        tenant_per_group, lengths, pltpu.with_memory_space_constraint(ranks, pltpu.HBM),
    )
    return projected, grad_x, jnp.swapaxes(up, 0, 1)[None]


def solution(mesh):
    placed = (
        P(("dp", "fsdp"), None),
        P(("dp", "fsdp"), None),
        P("fsdp", None),
        P("dp", "fsdp", None),
        P("dp", None, "fsdp"),
        P("dp"),
        P("dp", "fsdp"),
        P(),
    )
    return jax.shard_map(
        per_device,
        mesh=mesh,
        in_specs=placed,
        out_specs=(P(("dp", "fsdp"), None), P(("dp", "fsdp"), None), P("dp", None, "fsdp")),
        check_vma=False,
    )
```
